32 devices in a mesh: ctx: 8 (over z, y), ch: 4 (over x, core).
Axes of the slice: x: 2, y: 2, z: 4, core: 2. Of those that a mesh axis runs over, the one named last changes fastest.
Arguments:
- features: bfloat16 [1536, 4096], P('ctx', 'ch'), may hold values from -6 to 6
- w_in: bfloat16 [4096, 3, 2048], P('ctx', None, 'ch'), may hold values from -0.09375 to 0.09375
- short_filter: float32 [3, 3, 2048], P(None, None, 'ch'), may hold values from -3 to 3
- filter_spectrum: float32 [2, 1536, 2048], P(None, 'ctx', 'ch'), may hold values from -6 to 6
- out_grad: bfloat16 [1536, 4096], P('ctx'), may hold values from -0.059814453 to 0.059814453
Outputs:
- gated: bfloat16 [1536, 2048], P('ctx', 'ch')
- w_out_grad: float32 [4096, 2048], P('ctx', 'ch')
The draws below stay inside these ranges and needn't reach their ends.
All inputs are finite; a program needn't handle non-finite values.
Results may differ from the reference program's by a relative error of at most 0.0065.
Values may be sent and summed in bfloat16 or wider, within the bound.
No kernel may reach another device: no remote copies, remote signals or barrier semaphores. Data moves between devices by JAX's collectives and lax.ppermute only.
A program may use at most 128 MiB of HBM per device.

```python
import jax
import jax.numpy as jnp

D = 4096
L_DEV = 192
SHARDS = 8
SECTIONS = 3
CHANNELS = 2048
TOKENS = 1536


def strengthened(drawn, stream_key, source, target, shards_of, factor):
    owner, partner = [(jnp.arange(drawn.shape[axis_at]) // (drawn.shape[axis_at] // shards_of)).reshape([-1 if axis == axis_at else 1 for axis in range(drawn.ndim)]) for axis_at in (source, target)]
    chosen = jax.random.permutation(stream_key, shards_of)[partner]
    strong = (owner == chosen) | (owner == (partner + shards_of // 2) % shards_of)
    return jnp.where(strong, factor * drawn, drawn)


def block_scale(own_key, shape, shards, low, high):
    def one(axis_at, parts):
        draws = jax.random.uniform(jax.random.fold_in(jax.random.fold_in(own_key, 6), axis_at), (parts,), jnp.float32, low / len(shards), high / len(shards))
        return jnp.repeat(jnp.exp(draws), shape[axis_at] // parts).reshape((-1,) + (1,) * (len(shape) - axis_at - 1))

    gain = one(*shards[0])
    for cut in shards[1:]:
        gain = gain * one(*cut)
    return gain


def scatter_about(rng, extent, spread, limit, pieces=(), kind=jnp.bfloat16):
    factor_of = block_scale(rng, extent, pieces, -0.22, 0.18) if pieces else 1.0
    entries = jax.random.normal(rng, extent, jnp.float32) * spread * factor_of
    return jnp.minimum(jnp.maximum(entries, -limit), limit).astype(kind)


def noise_with(own_key, extent, spread, most, split, heavy, kind=jnp.bfloat16):
    array = spread * jax.random.normal(own_key, extent, jnp.float32)
    if split:
        array = array * block_scale(own_key, extent, split, -0.22, 0.18)
    return jnp.clip(strengthened(array, jax.random.fold_in(own_key, 3), *heavy), -most, most).astype(kind)


def setup_inputs(seed: int = 0) -> dict:
    splits = jax.random.split(jax.random.key(seed), 6)
    return {
        "features": scatter_about(splits[0], (TOKENS, D), 1.0, 6.0, ((0, 8), (1, 4))),
        "w_in": scatter_about(splits[1], (D, 3, CHANNELS), D ** -0.5, 0.09375, ((0, 8), (2, 4))),
        "short_filter": scatter_about(splits[2], (3, 3, CHANNELS), 0.6, 3.0, ((2, 4),), jnp.float32),
        "filter_spectrum": scatter_about(splits[3], (2, TOKENS, CHANNELS), 1.0, 6.0, ((1, 8), (2, 4)), jnp.float32),
        "out_grad": noise_with(splits[4], (TOKENS, D), 0.01, 0.059814453, ((0, 8),), (0, 1, 8, 2.0)),
    }


def reverse_bits(values, count):
    result = jnp.zeros_like(values)
    for level in range(count):
        result = result | (((values >> level) & 1) << (count - 1 - level))
    return result


def reference(features, w_in, short_filter, filter_spectrum, out_grad):
    projected = jnp.dot(features, w_in.reshape(D, 3 * CHANNELS), preferred_element_type=jnp.float32)
    projected = projected.astype(jnp.bfloat16).reshape(TOKENS, 3, CHANNELS)
    leading = jnp.zeros((2, 3, CHANNELS), jnp.bfloat16)
    extended = jnp.concatenate([leading, projected], axis=0).astype(jnp.float32)
    mixed = short_filter[0] * extended[2:] + short_filter[1] * extended[1:TOKENS + 1] + short_filter[2] * extended[:TOKENS]
    query = mixed[:, 0]
    signal = mixed[:, 1] * mixed[:, 2]
    frequency = jnp.arange(TOKENS, dtype=jnp.int32)
    source_rows = (reverse_bits(frequency % SHARDS, SECTIONS) * L_DEV + frequency // SHARDS).astype(jnp.int32)
    filter_real = jnp.take(filter_spectrum[0], source_rows, axis=0)
    filter_imag = jnp.take(filter_spectrum[1], source_rows, axis=0)
    spectrum = jnp.fft.fft(signal, axis=0)
    convolved = jnp.real(jnp.fft.ifft(spectrum * (filter_real + 1j * filter_imag), axis=0))
    gated = (query * convolved).astype(jnp.bfloat16)
    w_out_grad = jnp.dot(out_grad.T, gated, preferred_element_type=jnp.float32)
    return gated, w_out_grad
```

```python
import math

import jax
import jax.numpy as jnp
from jax import lax
from jax.sharding import PartitionSpec as P

TWO_PI = 2.0 * math.pi
BOTH = ("ctx", "ch")


def product(spec, left, right):
    return jnp.einsum(
        spec, left, right, precision=lax.Precision.HIGHEST, preferred_element_type=jnp.float32
    )


def reverse_bits(values, count):
    result = jnp.zeros_like(values)
    for level in range(count):
        result = result | (values >> level & 1) << count - 1 - level
    return result


def phase_tables(phase, period):
    angle = TWO_PI / period * phase.astype(jnp.float32)
    return (jnp.cos(angle), jnp.sin(angle))


def gather_pairs(value, n, place):
    pairs = n // 2
    odd = place % 2
    near = [value]
    for shift in range(1, pairs):
        hops = [(i, (i // 2 + shift) % pairs * 2 + i % 2) for i in range(n)]
        near.append(lax.ppermute(value, "ctx", hops))
    flips = [(i, i ^ 1) for i in range(n)]
    found = []
    for shift in range(pairs):
        other = lax.ppermute(near[shift], "ctx", flips)
        low = jnp.where(odd == 0, near[shift], other)
        high = jnp.where(odd == 0, other, near[shift])
        found.append(((place // 2 - shift) % pairs, low, high))
    return found


def on_device(features, w_in, short_filter, filter_spectrum, out_grad):
    n = lax.axis_size("ctx")
    m = lax.axis_size("ch")
    place = lax.axis_index("ctx")
    column = lax.axis_index("ch")
    rows, depth = features.shape
    total = rows * n
    share = n // m
    block_depth = w_in.shape[0]
    width = w_in.shape[2]
    own = width // n
    sections = n.bit_length() - 1

    whole = jnp.zeros((n // 2, 2, rows, depth), features.dtype)
    for index, low, high in gather_pairs(features, n, place):
        whole = lax.dynamic_update_slice(whole, jnp.stack([low, high])[None], (index, 0, 0, 0))
    whole = whole.reshape(total, depth)

    turned = w_in.reshape(block_depth, 3, n, own).transpose(2, 1, 3, 0)
    sender = place % share * m + column
    weights = jnp.zeros((n, 3, own, block_depth), w_in.dtype)
    for step in range(n):
        hops = []
        for i in range(n):
            for j in range(m):
                hops.append((i * m + j, (i % share * m + j + step) % n * m + i // share))
        piece = lax.dynamic_index_in_dim(turned, (sender + step) % n, 0)
        piece = lax.ppermute(piece, BOTH, hops)
        weights = lax.dynamic_update_slice(weights, piece, ((place - step) % n, 0, 0, 0))
    weights = weights.reshape(share, m * 3 * own, block_depth).transpose(1, 0, 2)
    weights = weights.reshape(m * 3 * own, depth)

    partial = lax.dot_general(
        weights, whole, (((1,), (1,)), ((), ())), preferred_element_type=jnp.float32
    )
    partial = partial.reshape(m, 3 * own, total)
    bits = m.bit_length() - 1
    for bit in range(bits):
        mine = column >> bit & 1
        halves = partial.reshape(-1, 2, 3 * own, total)
        keep = lax.dynamic_index_in_dim(halves, mine, 1, keepdims=False)
        send = lax.dynamic_index_in_dim(halves, 1 - mine, 1, keepdims=False)
        if bit == bits - 1:
            send = send.astype(jnp.bfloat16)
        flips = [(j, j ^ 1 << bit) for j in range(m)]
        partial = keep + lax.ppermute(send, "ch", flips).astype(jnp.float32)
    projected = partial.reshape(3, own, total).astype(jnp.bfloat16).astype(jnp.float32)

    taps = lax.dynamic_slice_in_dim(short_filter, place * own, own, 2)[:, :, :, None]
    padded = jnp.pad(projected, ((0, 0), (0, 0), (2, 0)))
    mixed = (
        taps[0] * projected + taps[1] * padded[:, :, 1 : total + 1] + taps[2] * padded[:, :, :total]
    )
    query = mixed[0]
    signal = (mixed[1] * mixed[2]).reshape(own, n, rows)

    response = lax.all_to_all(
        filter_spectrum.reshape(2, rows, n, own).transpose(2, 3, 0, 1),
        "ctx", split_axis=0, concat_axis=0, tiled=True,
    )
    grid = lax.broadcasted_iota(jnp.int32, (rows, rows), 0) * lax.broadcasted_iota(
        jnp.int32, (rows, rows), 1
    )
    local_cos, local_sin = phase_tables(grid % rows, rows)
    order = reverse_bits(lax.broadcasted_iota(jnp.int32, (n, 1), 0), sections)
    across = order * lax.broadcasted_iota(jnp.int32, (1, n), 1)
    across_cos, across_sin = phase_tables(across % n, n)
    turn = order * lax.broadcasted_iota(jnp.int32, (1, rows), 1)
    turn_cos, turn_sin = phase_tables(turn % total, total)
    turn_cos, turn_sin = turn_cos[:, None], turn_sin[:, None]
    real = product("rn,cnt->rct", across_cos, signal)
    imag = -product("rn,cnt->rct", across_sin, signal)
    real, imag = real * turn_cos + imag * turn_sin, imag * turn_cos - real * turn_sin
    spec_real = product("rct,tq->rcq", real, local_cos) + product("rct,tq->rcq", imag, local_sin)
    spec_imag = product("rct,tq->rcq", imag, local_cos) - product("rct,tq->rcq", real, local_sin)
    res_real, res_imag = response[:, :, 0], response[:, :, 1]
    prod_real = spec_real * res_real - spec_imag * res_imag
    prod_imag = spec_real * res_imag + spec_imag * res_real
    back_real = product("rcq,qt->rct", prod_real, local_cos) - product(
        "rcq,qt->rct", prod_imag, local_sin
    )
    back_imag = product("rcq,qt->rct", prod_imag, local_cos) + product(
        "rcq,qt->rct", prod_real, local_sin
    )
    back_real, back_imag = (
        back_real * turn_cos - back_imag * turn_sin,
        back_imag * turn_cos + back_real * turn_sin,
    )
    convolved = (
        product("rn,rct->cnt", across_cos, back_real)
        - product("rn,rct->cnt", across_sin, back_imag)
    ) / total
    gated = (query * convolved.reshape(own, total)).astype(jnp.bfloat16)

    out_rows = out_grad.shape[1] // n
    part = out_rows // m
    mine = lax.dynamic_index_in_dim(
        out_grad.reshape(rows, n, m, part), column, 2, keepdims=False
    )
    mine = lax.all_to_all(mine, "ctx", split_axis=1, concat_axis=0, tiled=True)
    grads = lax.all_gather(mine.reshape(total, part), "ch", axis=1, tiled=True)

    every = jnp.zeros((n // 2, 2, own, total), jnp.bfloat16)
    for index, low, high in gather_pairs(gated, n, place):
        every = lax.dynamic_update_slice(every, jnp.stack([low, high])[None], (index, 0, 0, 0))
    every = every.reshape(width, total)
    w_out_grad = lax.dot_general(
        grads, every, (((0,), (1,)), ((), ())), preferred_element_type=jnp.float32
    )
    out = lax.dynamic_slice_in_dim(every, place * rows, rows, 1).T
    return (out, w_out_grad)


def solution(mesh):
    in_specs = (
        P("ctx", "ch"),
        P("ctx", None, "ch"),
        P(None, None, "ch"),
        P(None, "ctx", "ch"),
        P("ctx", None),
    )
    out_specs = (P("ctx", "ch"), P("ctx", "ch"))
    return jax.shard_map(
        on_device, mesh=mesh, in_specs=in_specs, out_specs=out_specs, check_vma=False
    )
```

```python
import functools
import math

import jax
import jax.numpy as jnp
import numpy as np
from jax import lax
from jax.experimental import pallas as pl
from jax.experimental.pallas import tpu as pltpu
from jax.sharding import PartitionSpec as P

TWO_PI = 2.0 * math.pi
BOTH = ("ctx", "ch")
ORDER = (0, 4, 2, 6, 1, 5, 3, 7)


def product(spec, left, right):
    return jnp.einsum(
        spec, left, right, precision=lax.Precision.HIGHEST, preferred_element_type=jnp.float32
    )


def reverse_bits(values, count):
    result = jnp.zeros_like(values)
    for level in range(count):
        result = result | (values >> level & 1) << count - 1 - level
    return result


def phase_tables(phase, period):
    angle = TWO_PI / period * phase.astype(jnp.float32)
    return (jnp.cos(angle), jnp.sin(angle))


def gather_pairs(value, n, place):
    pairs = n // 2
    odd = place % 2
    near = [value]
    for shift in range(1, pairs):
        hops = [(i, (i // 2 + shift) % pairs * 2 + i % 2) for i in range(n)]
        near.append(lax.ppermute(value, "ctx", hops))
    flips = [(i, i ^ 1) for i in range(n)]
    found = []
    for shift in range(pairs):
        other = lax.ppermute(near[shift], "ctx", flips)
        low = jnp.where(odd == 0, near[shift], other)
        high = jnp.where(odd == 0, other, near[shift])
        found.append(((place // 2 - shift) % pairs, low, high))
    return found


def general(features, w_in, short_filter, filter_spectrum, out_grad):
    n = lax.axis_size("ctx")
    m = lax.axis_size("ch")
    place = lax.axis_index("ctx")
    column = lax.axis_index("ch")
    rows, depth = features.shape
    total = rows * n
    share = n // m
    block_depth = w_in.shape[0]
    width = w_in.shape[2]
    own = width // n
    sections = n.bit_length() - 1

    whole = jnp.zeros((n // 2, 2, rows, depth), features.dtype)
    for index, low, high in gather_pairs(features, n, place):
        whole = lax.dynamic_update_slice(whole, jnp.stack([low, high])[None], (index, 0, 0, 0))
    whole = whole.reshape(total, depth)

    turned = w_in.reshape(block_depth, 3, n, own).transpose(2, 1, 3, 0)
    sender = place % share * m + column
    weights = jnp.zeros((n, 3, own, block_depth), w_in.dtype)
    for step in range(n):
        hops = []
        for i in range(n):
            for j in range(m):
                hops.append((i * m + j, (i % share * m + j + step) % n * m + i // share))
        piece = lax.dynamic_index_in_dim(turned, (sender + step) % n, 0)
        piece = lax.ppermute(piece, BOTH, hops)
        weights = lax.dynamic_update_slice(weights, piece, ((place - step) % n, 0, 0, 0))
    weights = weights.reshape(share, m * 3 * own, block_depth).transpose(1, 0, 2)
    weights = weights.reshape(m * 3 * own, depth)

    partial = lax.dot_general(
        weights, whole, (((1,), (1,)), ((), ())), preferred_element_type=jnp.float32
    )
    partial = partial.reshape(m, 3 * own, total)
    bits = m.bit_length() - 1
    for bit in range(bits):
        mine = column >> bit & 1
        halves = partial.reshape(-1, 2, 3 * own, total)
        keep = lax.dynamic_index_in_dim(halves, mine, 1, keepdims=False)
        send = lax.dynamic_index_in_dim(halves, 1 - mine, 1, keepdims=False)
        if bit == bits - 1:
            send = send.astype(jnp.bfloat16)
        flips = [(j, j ^ 1 << bit) for j in range(m)]
        partial = keep + lax.ppermute(send, "ch", flips).astype(jnp.float32)
    projected = partial.reshape(3, own, total).astype(jnp.bfloat16).astype(jnp.float32)

    taps = lax.dynamic_slice_in_dim(short_filter, place * own, own, 2)[:, :, :, None]
    padded = jnp.pad(projected, ((0, 0), (0, 0), (2, 0)))
    mixed = (
        taps[0] * projected + taps[1] * padded[:, :, 1 : total + 1] + taps[2] * padded[:, :, :total]
    )
    query = mixed[0]
    signal = (mixed[1] * mixed[2]).reshape(own, n, rows)

    response = lax.all_to_all(
        filter_spectrum.reshape(2, rows, n, own).transpose(2, 3, 0, 1),
        "ctx", split_axis=0, concat_axis=0, tiled=True,
    )
    grid = lax.broadcasted_iota(jnp.int32, (rows, rows), 0) * lax.broadcasted_iota(
        jnp.int32, (rows, rows), 1
    )
    local_cos, local_sin = phase_tables(grid % rows, rows)
    order = reverse_bits(lax.broadcasted_iota(jnp.int32, (n, 1), 0), sections)
    across = order * lax.broadcasted_iota(jnp.int32, (1, n), 1)
    across_cos, across_sin = phase_tables(across % n, n)
    turn = order * lax.broadcasted_iota(jnp.int32, (1, rows), 1)
    turn_cos, turn_sin = phase_tables(turn % total, total)
    turn_cos, turn_sin = turn_cos[:, None], turn_sin[:, None]
    real = product("rn,cnt->rct", across_cos, signal)
    imag = -product("rn,cnt->rct", across_sin, signal)
    real, imag = real * turn_cos + imag * turn_sin, imag * turn_cos - real * turn_sin
    spec_real = product("rct,tq->rcq", real, local_cos) + product("rct,tq->rcq", imag, local_sin)
    spec_imag = product("rct,tq->rcq", imag, local_cos) - product("rct,tq->rcq", real, local_sin)
    res_real, res_imag = response[:, :, 0], response[:, :, 1]
    prod_real = spec_real * res_real - spec_imag * res_imag
    prod_imag = spec_real * res_imag + spec_imag * res_real
    back_real = product("rcq,qt->rct", prod_real, local_cos) - product(
        "rcq,qt->rct", prod_imag, local_sin
    )
    back_imag = product("rcq,qt->rct", prod_imag, local_cos) + product(
        "rcq,qt->rct", prod_real, local_sin
    )
    back_real, back_imag = (
        back_real * turn_cos - back_imag * turn_sin,
        back_imag * turn_cos + back_real * turn_sin,
    )
    convolved = (
        product("rn,rct->cnt", across_cos, back_real)
        - product("rn,rct->cnt", across_sin, back_imag)
    ) / total
    gated = (query * convolved.reshape(own, total)).astype(jnp.bfloat16)

    out_rows = out_grad.shape[1] // n
    part = out_rows // m
    mine = lax.dynamic_index_in_dim(
        out_grad.reshape(rows, n, m, part), column, 2, keepdims=False
    )
    mine = lax.all_to_all(mine, "ctx", split_axis=1, concat_axis=0, tiled=True)
    grads = lax.all_gather(mine.reshape(total, part), "ch", axis=1, tiled=True)

    every = jnp.zeros((n // 2, 2, own, total), jnp.bfloat16)
    for index, low, high in gather_pairs(gated, n, place):
        every = lax.dynamic_update_slice(every, jnp.stack([low, high])[None], (index, 0, 0, 0))
    every = every.reshape(width, total)
    w_out_grad = lax.dot_general(
        grads, every, (((0,), (1,)), ((), ())), preferred_element_type=jnp.float32
    )
    out = lax.dynamic_slice_in_dim(every, place * rows, rows, 1).T
    return (out, w_out_grad)


def exact(left, right):
    return jnp.dot(left, right, precision=lax.Precision.HIGHEST, preferred_element_type=jnp.float32)

def tables(rows, lanes):
    grid = np.arange(rows)[:, None] * np.arange(rows)[None, :] % rows
    angle = 2.0 * math.pi / rows * grid
    table = np.zeros((rows, 2 * lanes), np.float32)
    table[:, :rows] = np.cos(angle)
    table[:, lanes : lanes + rows] = np.sin(angle)
    turn = 2.0 * math.pi / (8 * rows) * (np.arange(5)[:, None] * np.arange(rows)[None, :])
    return table, np.stack([np.cos(turn), np.sin(turn)]).astype(np.float32)

def convolve_kernel(odd_ref, mine_ref, other_ref, taps_ref, response_ref, table_ref, turn_ref, out_ref):
    own, total = out_ref.shape
    rows = total // 8
    lanes = table_ref.shape[1] // 2
    mine, other = mine_ref[...].astype(jnp.float32), other_ref[...].astype(jnp.float32)
    even, uneven = jnp.where(odd_ref[0] == 0, mine, other), jnp.where(odd_ref[0] == 0, other, mine)
    slabs = []
    for spot in range(4):
        slabs += [even[:, rows * spot : rows * (spot + 1)], uneven[:, rows * spot : rows * (spot + 1)]]
    projected = jnp.concatenate(slabs, axis=1)
    lane = lax.broadcasted_iota(jnp.int32, projected.shape, 1)
    mixed = taps_ref[0] * projected
    for back in (1, 2):
        moved = jnp.where(lane < back, 0.0, pltpu.roll(projected, back, 1))
        mixed += taps_ref[back] * moved
    query = mixed[:own]
    signal = mixed[own : 2 * own] * mixed[2 * own :]
    a = [signal[:, rows * i : rows * (i + 1)] for i in range(8)]
    half = math.sqrt(0.5)
    s04, d04, s26, d26 = a[0] + a[4], a[0] - a[4], a[2] + a[6], a[2] - a[6]
    s15, d15, s37, d37 = a[1] + a[5], a[1] - a[5], a[3] + a[7], a[3] - a[7]
    e, f = s04 + s26, s15 + s37
    g, h = half * (d15 - d37), half * (d15 + d37)
    real = [e + f, d04 + g, s04 - s26, d04 - g, e - f]
    imag = [None, -(d26 + h), s37 - s15, d26 - h, None]
    ins = [real[0]]
    for r in range(1, 5):
        cos, sin = turn_ref[0, r : r + 1], turn_ref[1, r : r + 1]
        if imag[r] is None:
            ins += [real[r] * cos, -real[r] * sin]
        else:
            ins += [real[r] * cos + imag[r] * sin, imag[r] * cos - real[r] * sin]
    spectrum = exact(jnp.concatenate(ins, axis=0), table_ref[...])
    response = [
        jnp.concatenate([response_ref[ORDER[r], i] for i in range(response_ref.shape[1])], axis=1)
        for r in range(8)
    ]
    response = [value.astype(jnp.float32) for value in response]
    outs = []
    for r in range(5):
        if r == 0:
            first = spectrum[:own]
            spec_real, spec_imag = first[:, :rows], -first[:, lanes : lanes + rows]
        else:
            first = spectrum[(2 * r - 1) * own : 2 * r * own]
            second = spectrum[2 * r * own : (2 * r + 1) * own]
            spec_real = first[:, :rows] + second[:, lanes : lanes + rows]
            spec_imag = second[:, :rows] - first[:, lanes : lanes + rows]
        own_class = response[r]
        res_real, res_imag = own_class[:, :rows], own_class[:, rows:]
        if r in (1, 2, 3):
            mirrored = response[8 - r]
            res_real = 0.5 * (res_real + mirrored[:, :rows])
            res_imag = 0.5 * (res_imag - mirrored[:, rows:])
        outs += [spec_real * res_real - spec_imag * res_imag, spec_real * res_imag + spec_imag * res_real]
    back = exact(jnp.concatenate(outs, axis=0), table_ref[...])
    u_real, u_imag = [], []
    for r in range(5):
        first = back[2 * r * own : (2 * r + 1) * own]
        second = back[(2 * r + 1) * own : (2 * r + 2) * own]
        v_real = first[:, :rows] - second[:, lanes : lanes + rows]
        if r == 0:
            u_real.append(v_real)
            u_imag.append(None)
            continue
        v_imag = second[:, :rows] + first[:, lanes : lanes + rows]
        cos, sin = turn_ref[0, r : r + 1], turn_ref[1, r : r + 1]
        u_real.append(v_real * cos - v_imag * sin)
        u_imag.append(None if r == 4 else v_imag * cos + v_real * sin)
    p, q = u_real[0] + u_real[4], u_real[0] - u_real[4]
    r13, i13 = u_real[1] + u_real[3], u_imag[1] - u_imag[3]
    dr, di = half * (u_real[1] - u_real[3]), half * (u_imag[1] + u_imag[3])
    two = 2.0
    r2, i2 = u_real[2], u_imag[2]
    y = [p + two * (r13 + r2), q + two * (dr - di - i2), p - two * (i13 + r2), q + two * (i2 - dr - di),
         p + two * (r2 - r13), q + two * (di - dr - i2), p + two * (i13 - r2), q + two * (dr + di + i2)]
    scale = 1.0 / total
    convolved = jnp.concatenate(y, axis=1) * scale
    out_ref[...] = (query * convolved).astype(jnp.bfloat16)

def convolve(odd, mine, other, taps, response):
    total = 2 * mine.shape[1]
    own = mine.shape[0] // 3
    rows = total // 8
    table, turn = tables(rows, -(-rows // 128) * 128)
    return pl.pallas_call(convolve_kernel, out_shape=jax.ShapeDtypeStruct((own, total), jnp.bfloat16),
        in_specs=[pl.BlockSpec(memory_space=pltpu.SMEM)] + [pl.BlockSpec(memory_space=pltpu.VMEM)] * 6,
        compiler_params=pltpu.CompilerParams(vmem_limit_bytes=48*2**20),
        cost_estimate=pl.CostEstimate(flops=10**9, bytes_accessed=4*10**6, transcendentals=0),
    )(odd, mine, other, taps, response, jnp.asarray(table), jnp.asarray(turn))


PARTS = 2


def multiply_kernel(part, slots, whole_ref, *refs):
    send_ref, keep_ref, held, sems = refs[-4:]
    pieces = refs[:-4]
    share, spots, spot, block_depth = held.shape
    copies = []
    for step, piece in enumerate(pieces):
        copies.append(
            pltpu.make_async_copy(
                piece.at[pl.ds(part * spot, spot)],
                held.at[slots[0, step], slots[1, step]],
                sems.at[step],
            )
        )
    for copy in copies:
        copy.start()
    for copy in copies:
        copy.wait()
    for place in (1, 3, 2, 0):
        total = jnp.zeros((spot, whole_ref.shape[0]), jnp.float32)
        for block in range(share):
            total += lax.dot_general(
                held[block, place],
                whole_ref[:, block * block_depth : (block + 1) * block_depth],
                (((1,), (1,)), ((), ())),
                preferred_element_type=jnp.float32,
            )
        out_ref = send_ref if place % 2 else keep_ref
        out_ref[place // 2] = total


def multiply(part, slots, whole, pieces, share):
    rows, block_depth = pieces[0].shape
    spot = rows // PARTS
    spots = len(pieces) // share
    vmem = pl.BlockSpec(memory_space=pltpu.VMEM)
    anywhere = pl.BlockSpec(memory_space=pl.ANY)
    out = jax.ShapeDtypeStruct((spots // 2, spot, whole.shape[0]), jnp.float32)
    return pl.pallas_call(
        functools.partial(multiply_kernel, part),
        out_shape=[out] * 2,
        in_specs=[pl.BlockSpec(memory_space=pltpu.SMEM), vmem] + [anywhere] * len(pieces),
        out_specs=[vmem] * 2,
        scratch_shapes=[
            pltpu.VMEM((share, spots, spot, block_depth), jnp.bfloat16),
            pltpu.SemaphoreType.DMA((len(pieces),)),
        ],
        compiler_params=pltpu.CompilerParams(vmem_limit_bytes=32 * 2**20),
        cost_estimate=pl.CostEstimate(
            flops=2 * spots * spot * whole.shape[0] * whole.shape[1],
            bytes_accessed=6 * 2**20,
            transcendentals=0,
        ),
    )(slots, whole, *pieces)


def pack_kernel(flag_ref, value_ref, grad_ref, out_ref):
    rows = value_ref.shape[1]
    n, _, count, lanes = out_ref.shape
    own = value_ref.shape[2] // n
    down = lax.broadcasted_iota(jnp.int32, (rows, rows), 0)
    along = lax.broadcasted_iota(jnp.int32, (rows, rows), 1)
    target = jnp.where(flag_ref[0] == 1, rows - 1 - down, down)
    swap = (along == target).astype(jnp.bfloat16)
    turned = [
        lax.dot_general(
            value_ref[part].astype(jnp.bfloat16),
            swap,
            (((0,), (0,)), ((), ())),
            preferred_element_type=jnp.float32,
        ).astype(jnp.bfloat16)
        for part in range(2)
    ]
    turned = jnp.concatenate(turned, axis=1)
    step = grad_ref.shape[1] // n
    for place in range(n):
        for chunk in range(count // own):
            out_ref[place, 0, own * chunk : own * (chunk + 1)] = turned[
                own * place : own * (place + 1), lanes * chunk : lanes * (chunk + 1)
            ]
        start = pl.multiple_of(place * step + flag_ref[1] * lanes, lanes)
        out_ref[place, 1] = grad_ref[:, pl.ds(start, lanes)]


def pack(flags, value, grad, n, m):
    rows = grad.shape[0]
    lanes = grad.shape[1] // (n * m)
    vmem = pl.BlockSpec(memory_space=pltpu.VMEM)
    return pl.pallas_call(
        pack_kernel,
        out_shape=jax.ShapeDtypeStruct((n, 2, rows, lanes), jnp.bfloat16),
        in_specs=[pl.BlockSpec(memory_space=pltpu.SMEM), vmem, vmem],
        out_specs=vmem,
        compiler_params=pltpu.CompilerParams(vmem_limit_bytes=32 * 2**20),
        cost_estimate=pl.CostEstimate(flops=10**8, bytes_accessed=4 * 2**20, transcendentals=0),
    )(flags, value, grad)


def fits(mesh):
    return mesh.shape["ctx"] == 8 and mesh.shape["ch"] == 4


def after(value, *others):
    return lax.optimization_barrier((value, *others))[0]


def special(features, w_in, short_filter, filter_spectrum, out_grad):
    n = lax.axis_size("ctx")
    m = lax.axis_size("ch")
    place = lax.axis_index("ctx")
    column = lax.axis_index("ch")
    rows, depth = features.shape
    total = rows * n
    share = n // m
    pairs = n // 2
    line = place // 2
    odd = place % 2
    block_depth = w_in.shape[0]
    width = w_in.shape[2]
    own = width // n
    sub = own // PARTS
    sections = n.bit_length() - 1
    flips = [(i, i ^ 1) for i in range(n)]
    shifts = [[(i, (i // 2 + s) % pairs * 2 + i % 2) for i in range(n)] for s in range(pairs)]
    up = [(i, i + 2) for i in range(n - 2)]
    down = [(i + 2, i) for i in range(n - 2)]

    def trade(value, bit):
        return lax.ppermute(value, "ch", [(j, j ^ 1 << bit) for j in range(m)])

    up1 = lax.ppermute(features, "ctx", up)
    down1 = lax.ppermute(features, "ctx", down)

    turned = w_in.reshape(block_depth, 3, pairs, 2, PARTS, sub).transpose(2, 4, 3, 1, 5, 0)
    turned = turned.reshape(pairs, PARTS * 2 * 3 * sub, block_depth)
    pieces = []
    for step in range(m):
        hops = []
        for i in range(n):
            for j in range(m):
                hops.append((i * m + j, ((j + step) % m * 2 + i % 2) * m + i // 2))
        piece = lax.dynamic_index_in_dim(turned, (column + step) % m, 0, keepdims=False)
        if step >= m // 2:
            piece = after(piece, up1, down1)
        pieces.append(lax.ppermute(piece, BOTH, hops))
    pieces += [lax.ppermute(piece, "ctx", flips) for piece in pieces]

    mirrored = (reverse_bits(place, sections) > n // 2).astype(jnp.int32)
    packed = pack(jnp.stack([mirrored, column]), filter_spectrum, out_grad, n, m)

    up2 = lax.ppermute(up1, "ctx", up)
    down2 = lax.ppermute(down1, "ctx", down)
    up3 = lax.ppermute(after(up2, packed), "ctx", up)
    down3 = lax.ppermute(after(down2, packed), "ctx", down)
    behind = [
        jnp.where(line >= 1, up1, down3),
        jnp.where(line >= 2, up2, down2),
        jnp.where(line >= 3, up3, down1),
    ]
    whole = jnp.zeros((pairs, rows, depth), features.dtype)
    for shift, value in enumerate([features] + behind):
        whole = lax.dynamic_update_slice(whole, value[None], ((line - shift) % pairs, 0, 0))
    whole = whole.reshape(pairs * rows, depth)

    sources = (line - jnp.arange(m, dtype=jnp.int32)) % m ^ column
    blocks = jnp.concatenate([jnp.full((m,), odd), jnp.full((m,), 1 - odd)])
    slots = jnp.stack([blocks, jnp.concatenate([sources, sources])])

    packed = after(packed, up3, down3, *pieces[:m])
    packed = lax.all_to_all(packed, "ctx", split_axis=0, concat_axis=0, tiled=True)
    response = packed[:, 0].reshape(n, rows // own, own, packed.shape[3])

    taps = lax.dynamic_slice_in_dim(short_filter, place * own, own, 2)
    taps = taps.reshape(3, 3, PARTS, sub).transpose(2, 0, 1, 3).reshape(PARTS, 3, 3 * sub, 1)
    sends, keeps = zip(*[multiply(part, slots, whole, pieces, share) for part in range(PARTS)])
    gots = [trade(send, 0) for send in sends]
    across = [
        trade((keep[1] + got[1]).astype(jnp.bfloat16), 1) for keep, got in zip(keeps, gots)
    ]
    gated = []
    for part in range(PARTS):
        projected = keeps[part][0] + gots[part][0] + across[part].astype(jnp.float32)
        projected = projected.astype(jnp.bfloat16).reshape(2, 3 * sub, total // 2)
        mine = lax.dynamic_index_in_dim(projected, odd, 0, keepdims=False)
        give = lax.dynamic_index_in_dim(projected, 1 - odd, 0, keepdims=False)
        other = lax.ppermute(give, "ctx", flips)
        gated.append(
            convolve(
                odd.reshape(1), mine, other, taps[part],
                response[:, :, part * sub : (part + 1) * sub],
            )
        )

    grads = packed[:, 1].reshape(total, packed.shape[3])
    for bit in (1, 0):
        other = trade(grads, bit)
        low = column >> bit & 1 == 0
        if bit == 1:
            grads = jnp.stack([jnp.where(low, grads, other), jnp.where(low, other, grads)])
        else:
            low, high = jnp.where(low, grads, other), jnp.where(low, other, grads)
            grads = jnp.concatenate([low[0], high[0], low[1], high[1]], axis=1)

    every = jnp.zeros((pairs, 2, PARTS, sub, total), jnp.bfloat16)
    for part in range(PARTS):
        near = [gated[part]]
        near += [lax.ppermute(gated[part], "ctx", shifts[s]) for s in range(1, pairs)]
        near = jnp.stack(near)
        other = lax.ppermute(near, "ctx", flips)
        low = jnp.where(odd == 0, near, other)
        high = jnp.where(odd == 0, other, near)
        for shift in range(pairs):
            every = lax.dynamic_update_slice(
                every,
                jnp.stack([low[shift], high[shift]])[None, :, None],
                ((line - shift) % pairs, 0, part, 0, 0),
            )
    every = every.reshape(width, total)
    w_out_grad = lax.dot_general(
        grads, every, (((0,), (1,)), ((), ())), preferred_element_type=jnp.float32
    )
    out = lax.dynamic_slice_in_dim(every, place * rows, rows, 1).T
    return (out, w_out_grad)


def solution(mesh):
    in_specs = (
        P("ctx", "ch"),
        P("ctx", None, "ch"),
        P(None, None, "ch"),
        P(None, "ctx", "ch"),
        P("ctx", None),
    )
    out_specs = (P("ctx", "ch"), P("ctx", "ch"))
    on_device = special if fits(mesh) else general
    return jax.shard_map(
        on_device, mesh=mesh, in_specs=in_specs, out_specs=out_specs, check_vma=False
    )
```

```python
import functools
import math

import jax
import jax.numpy as jnp
import numpy as np
from jax import lax
from jax.experimental import pallas as pl
from jax.experimental.pallas import tpu as pltpu
from jax.sharding import PartitionSpec as P

TWO_PI = 2.0 * math.pi
BOTH = ("ctx", "ch")
ORDER = (0, 4, 2, 6, 1, 5, 3, 7)


def product(spec, left, right):
    return jnp.einsum(
        spec, left, right, precision=lax.Precision.HIGHEST, preferred_element_type=jnp.float32
    )


def reverse_bits(values, count):
    result = jnp.zeros_like(values)
    for level in range(count):
        result = result | (values >> level & 1) << count - 1 - level
    return result


def phase_tables(phase, period):
    angle = TWO_PI / period * phase.astype(jnp.float32)
    return (jnp.cos(angle), jnp.sin(angle))


def gather_pairs(value, n, place):
    pairs = n // 2
    odd = place % 2
    near = [value]
    for shift in range(1, pairs):
        hops = [(i, (i // 2 + shift) % pairs * 2 + i % 2) for i in range(n)]
        near.append(lax.ppermute(value, "ctx", hops))
    flips = [(i, i ^ 1) for i in range(n)]
    found = []
    for shift in range(pairs):
        other = lax.ppermute(near[shift], "ctx", flips)
        low = jnp.where(odd == 0, near[shift], other)
        high = jnp.where(odd == 0, other, near[shift])
        found.append(((place // 2 - shift) % pairs, low, high))
    return found


def general(features, w_in, short_filter, filter_spectrum, out_grad):
    n = lax.axis_size("ctx")
    m = lax.axis_size("ch")
    place = lax.axis_index("ctx")
    column = lax.axis_index("ch")
    rows, depth = features.shape
    total = rows * n
    share = n // m
    block_depth = w_in.shape[0]
    width = w_in.shape[2]
    own = width // n
    sections = n.bit_length() - 1

    whole = jnp.zeros((n // 2, 2, rows, depth), features.dtype)
    for index, low, high in gather_pairs(features, n, place):
        whole = lax.dynamic_update_slice(whole, jnp.stack([low, high])[None], (index, 0, 0, 0))
    whole = whole.reshape(total, depth)

    turned = w_in.reshape(block_depth, 3, n, own).transpose(2, 1, 3, 0)
    sender = place % share * m + column
    weights = jnp.zeros((n, 3, own, block_depth), w_in.dtype)
    for step in range(n):
        hops = []
        for i in range(n):
            for j in range(m):
                hops.append((i * m + j, (i % share * m + j + step) % n * m + i // share))
        piece = lax.dynamic_index_in_dim(turned, (sender + step) % n, 0)
        piece = lax.ppermute(piece, BOTH, hops)
        weights = lax.dynamic_update_slice(weights, piece, ((place - step) % n, 0, 0, 0))
    weights = weights.reshape(share, m * 3 * own, block_depth).transpose(1, 0, 2)
    weights = weights.reshape(m * 3 * own, depth)

    partial = lax.dot_general(
        weights, whole, (((1,), (1,)), ((), ())), preferred_element_type=jnp.float32
    )
    partial = partial.reshape(m, 3 * own, total)
    bits = m.bit_length() - 1
    for bit in range(bits):
        mine = column >> bit & 1
        halves = partial.reshape(-1, 2, 3 * own, total)
        keep = lax.dynamic_index_in_dim(halves, mine, 1, keepdims=False)
        send = lax.dynamic_index_in_dim(halves, 1 - mine, 1, keepdims=False)
        if bit == bits - 1:
            send = send.astype(jnp.bfloat16)
        flips = [(j, j ^ 1 << bit) for j in range(m)]
        partial = keep + lax.ppermute(send, "ch", flips).astype(jnp.float32)
    projected = partial.reshape(3, own, total).astype(jnp.bfloat16).astype(jnp.float32)

    taps = lax.dynamic_slice_in_dim(short_filter, place * own, own, 2)[:, :, :, None]
    padded = jnp.pad(projected, ((0, 0), (0, 0), (2, 0)))
    mixed = (
        taps[0] * projected + taps[1] * padded[:, :, 1 : total + 1] + taps[2] * padded[:, :, :total]
    )
    query = mixed[0]
    signal = (mixed[1] * mixed[2]).reshape(own, n, rows)

    response = lax.all_to_all(
        filter_spectrum.reshape(2, rows, n, own).transpose(2, 3, 0, 1),
        "ctx", split_axis=0, concat_axis=0, tiled=True,
    )
    grid = lax.broadcasted_iota(jnp.int32, (rows, rows), 0) * lax.broadcasted_iota(
        jnp.int32, (rows, rows), 1
    )
    local_cos, local_sin = phase_tables(grid % rows, rows)
    order = reverse_bits(lax.broadcasted_iota(jnp.int32, (n, 1), 0), sections)
    across = order * lax.broadcasted_iota(jnp.int32, (1, n), 1)
    across_cos, across_sin = phase_tables(across % n, n)
    turn = order * lax.broadcasted_iota(jnp.int32, (1, rows), 1)
    turn_cos, turn_sin = phase_tables(turn % total, total)
    turn_cos, turn_sin = turn_cos[:, None], turn_sin[:, None]
    real = product("rn,cnt->rct", across_cos, signal)
    imag = -product("rn,cnt->rct", across_sin, signal)
    real, imag = real * turn_cos + imag * turn_sin, imag * turn_cos - real * turn_sin
    spec_real = product("rct,tq->rcq", real, local_cos) + product("rct,tq->rcq", imag, local_sin)
    spec_imag = product("rct,tq->rcq", imag, local_cos) - product("rct,tq->rcq", real, local_sin)
    res_real, res_imag = response[:, :, 0], response[:, :, 1]
    prod_real = spec_real * res_real - spec_imag * res_imag
    prod_imag = spec_real * res_imag + spec_imag * res_real
    back_real = product("rcq,qt->rct", prod_real, local_cos) - product(
        "rcq,qt->rct", prod_imag, local_sin
    )
    back_imag = product("rcq,qt->rct", prod_imag, local_cos) + product(
        "rcq,qt->rct", prod_real, local_sin
    )
    back_real, back_imag = (
        back_real * turn_cos - back_imag * turn_sin,
        back_imag * turn_cos + back_real * turn_sin,
    )
    convolved = (
        product("rn,rct->cnt", across_cos, back_real)
        - product("rn,rct->cnt", across_sin, back_imag)
    ) / total
    gated = (query * convolved.reshape(own, total)).astype(jnp.bfloat16)

    out_rows = out_grad.shape[1] // n
    part = out_rows // m
    mine = lax.dynamic_index_in_dim(
        out_grad.reshape(rows, n, m, part), column, 2, keepdims=False
    )
    mine = lax.all_to_all(mine, "ctx", split_axis=1, concat_axis=0, tiled=True)
    grads = lax.all_gather(mine.reshape(total, part), "ch", axis=1, tiled=True)

    every = jnp.zeros((n // 2, 2, own, total), jnp.bfloat16)
    for index, low, high in gather_pairs(gated, n, place):
        every = lax.dynamic_update_slice(every, jnp.stack([low, high])[None], (index, 0, 0, 0))
    every = every.reshape(width, total)
    w_out_grad = lax.dot_general(
        grads, every, (((0,), (1,)), ((), ())), preferred_element_type=jnp.float32
    )
    out = lax.dynamic_slice_in_dim(every, place * rows, rows, 1).T
    return (out, w_out_grad)


def exact(left, right):
    return jnp.dot(left, right, precision=lax.Precision.HIGHEST, preferred_element_type=jnp.float32)

def tables(rows, lanes):
    grid = np.arange(rows)[:, None] * np.arange(rows)[None, :] % rows
    angle = 2.0 * math.pi / rows * grid
    table = np.zeros((rows, 2 * lanes), np.float32)
    table[:, :rows] = np.cos(angle)
    table[:, lanes : lanes + rows] = np.sin(angle)
    turn = 2.0 * math.pi / (8 * rows) * (np.arange(5)[:, None] * np.arange(rows)[None, :])
    return table, np.stack([np.cos(turn), np.sin(turn)]).astype(np.float32)

def convolve_kernel(odd_ref, mine_ref, other_ref, taps_ref, response_ref, table_ref, turn_ref, out_ref):
    own, total = out_ref.shape
    rows = total // 8
    lanes = table_ref.shape[1] // 2
    mine, other = mine_ref[...].astype(jnp.float32), other_ref[...].astype(jnp.float32)
    even, uneven = jnp.where(odd_ref[0] == 0, mine, other), jnp.where(odd_ref[0] == 0, other, mine)
    slabs = []
    for spot in range(4):
        slabs += [even[:, rows * spot : rows * (spot + 1)], uneven[:, rows * spot : rows * (spot + 1)]]
    projected = jnp.concatenate(slabs, axis=1)
    lane = lax.broadcasted_iota(jnp.int32, projected.shape, 1)
    mixed = taps_ref[0] * projected
    for back in (1, 2):
        moved = jnp.where(lane < back, 0.0, pltpu.roll(projected, back, 1))
        mixed += taps_ref[back] * moved
    query = mixed[:own]
    signal = mixed[own : 2 * own] * mixed[2 * own :]
    a = [signal[:, rows * i : rows * (i + 1)] for i in range(8)]
    half = math.sqrt(0.5)
    s04, d04, s26, d26 = a[0] + a[4], a[0] - a[4], a[2] + a[6], a[2] - a[6]
    s15, d15, s37, d37 = a[1] + a[5], a[1] - a[5], a[3] + a[7], a[3] - a[7]
    e, f = s04 + s26, s15 + s37
    g, h = half * (d15 - d37), half * (d15 + d37)
    real = [e + f, d04 + g, s04 - s26, d04 - g, e - f]
    imag = [None, -(d26 + h), s37 - s15, d26 - h, None]
    ins = [real[0]]
    for r in range(1, 5):
        cos, sin = turn_ref[0, r : r + 1], turn_ref[1, r : r + 1]
        if imag[r] is None:
            ins += [real[r] * cos, -real[r] * sin]
        else:
            ins += [real[r] * cos + imag[r] * sin, imag[r] * cos - real[r] * sin]
    spectrum = exact(jnp.concatenate(ins, axis=0), table_ref[...])
    response = [
        jnp.concatenate([response_ref[odd_ref[1 + r], i] for i in range(response_ref.shape[1])], axis=1)
        for r in range(8)
    ]
    response = [value.astype(jnp.float32) for value in response]
    outs = []
    for r in range(5):
        if r == 0:
            first = spectrum[:own]
            spec_real, spec_imag = first[:, :rows], -first[:, lanes : lanes + rows]
        else:
            first = spectrum[(2 * r - 1) * own : 2 * r * own]
            second = spectrum[2 * r * own : (2 * r + 1) * own]
            spec_real = first[:, :rows] + second[:, lanes : lanes + rows]
            spec_imag = second[:, :rows] - first[:, lanes : lanes + rows]
        own_class = response[r]
        res_real, res_imag = own_class[:, :rows], own_class[:, rows:]
        if r in (1, 2, 3):
            mirrored = response[8 - r]
            res_real = 0.5 * (res_real + mirrored[:, :rows])
            res_imag = 0.5 * (res_imag - mirrored[:, rows:])
        outs += [spec_real * res_real - spec_imag * res_imag, spec_real * res_imag + spec_imag * res_real]
    back = exact(jnp.concatenate(outs, axis=0), table_ref[...])
    u_real, u_imag = [], []
    for r in range(5):
        first = back[2 * r * own : (2 * r + 1) * own]
        second = back[(2 * r + 1) * own : (2 * r + 2) * own]
        v_real = first[:, :rows] - second[:, lanes : lanes + rows]
        if r == 0:
            u_real.append(v_real)
            u_imag.append(None)
            continue
        v_imag = second[:, :rows] + first[:, lanes : lanes + rows]
        cos, sin = turn_ref[0, r : r + 1], turn_ref[1, r : r + 1]
        u_real.append(v_real * cos - v_imag * sin)
        u_imag.append(None if r == 4 else v_imag * cos + v_real * sin)
    p, q = u_real[0] + u_real[4], u_real[0] - u_real[4]
    r13, i13 = u_real[1] + u_real[3], u_imag[1] - u_imag[3]
    dr, di = half * (u_real[1] - u_real[3]), half * (u_imag[1] + u_imag[3])
    two = 2.0
    r2, i2 = u_real[2], u_imag[2]
    y = [p + two * (r13 + r2), q + two * (dr - di - i2), p - two * (i13 + r2), q + two * (i2 - dr - di),
         p + two * (r2 - r13), q + two * (di - dr - i2), p + two * (i13 - r2), q + two * (dr + di + i2)]
    scale = 1.0 / total
    convolved = jnp.concatenate(y, axis=1) * scale
    out_ref[...] = (query * convolved).astype(jnp.bfloat16)

def convolve(odd, mine, other, taps, response):
    total = 2 * mine.shape[1]
    own = mine.shape[0] // 3
    rows = total // 8
    table, turn = tables(rows, -(-rows // 128) * 128)
    return pl.pallas_call(convolve_kernel, out_shape=jax.ShapeDtypeStruct((own, total), jnp.bfloat16),
        in_specs=[pl.BlockSpec(memory_space=pltpu.SMEM)] + [pl.BlockSpec(memory_space=pltpu.VMEM)] * 6,
        compiler_params=pltpu.CompilerParams(vmem_limit_bytes=48*2**20),
        cost_estimate=pl.CostEstimate(flops=10**9, bytes_accessed=4*10**6, transcendentals=0),
    )(odd, mine, other, taps, response, jnp.asarray(table), jnp.asarray(turn))


PARTS = 2


def pack_kernel(flag_ref, value_ref, grad_ref, out_ref):
    rows = value_ref.shape[1]
    n, _, count, lanes = out_ref.shape
    own = value_ref.shape[2] // n
    down = lax.broadcasted_iota(jnp.int32, (rows, rows), 0)
    along = lax.broadcasted_iota(jnp.int32, (rows, rows), 1)
    target = jnp.where(flag_ref[0] == 1, rows - 1 - down, down)
    swap = (along == target).astype(jnp.bfloat16)
    turned = [
        lax.dot_general(
            value_ref[part].astype(jnp.bfloat16),
            swap,
            (((0,), (0,)), ((), ())),
            preferred_element_type=jnp.float32,
        ).astype(jnp.bfloat16)
        for part in range(2)
    ]
    turned = jnp.concatenate(turned, axis=1)
    step = grad_ref.shape[1] // n
    for place in range(n):
        for chunk in range(count // own):
            out_ref[place, 0, own * chunk : own * (chunk + 1)] = turned[
                own * place : own * (place + 1), lanes * chunk : lanes * (chunk + 1)
            ]
        start = pl.multiple_of(place * step + flag_ref[1] * lanes, lanes)
        out_ref[place, 1] = grad_ref[:, pl.ds(start, lanes)]


def pack(flags, value, grad, n, m):
    rows = grad.shape[0]
    lanes = grad.shape[1] // (n * m)
    vmem = pl.BlockSpec(memory_space=pltpu.VMEM)
    return pl.pallas_call(
        pack_kernel,
        out_shape=jax.ShapeDtypeStruct((n, 2, rows, lanes), jnp.bfloat16),
        in_specs=[pl.BlockSpec(memory_space=pltpu.SMEM), vmem, vmem],
        out_specs=vmem,
        compiler_params=pltpu.CompilerParams(vmem_limit_bytes=32 * 2**20),
        cost_estimate=pl.CostEstimate(flops=10**8, bytes_accessed=4 * 2**20, transcendentals=0),
    )(flags, value, grad)


def cut_kernel(step, which_ref, value_ref, *outs):
    kinds, _, width = value_ref.shape
    size = width // len(outs)
    for index, out_ref in enumerate(outs):
        start = pl.multiple_of(which_ref[index] * size, size)
        for kind in range(kinds):
            piece = value_ref[kind, :, pl.ds(start, size)].T
            for group in range(size // step):
                place = group % PARTS * 2 + group // PARTS
                first = (place * kinds + kind) * step
                out_ref[first : first + step] = piece[group * step : (group + 1) * step]


def cut(step, which, value):
    kinds, deep, width = value.shape
    vmem = pl.BlockSpec(memory_space=pltpu.VMEM)
    count = which.shape[0]
    out = jax.ShapeDtypeStruct((kinds * width // count, deep), value.dtype)
    return pl.pallas_call(
        functools.partial(cut_kernel, step),
        out_shape=[out] * count,
        in_specs=[pl.BlockSpec(memory_space=pltpu.SMEM), vmem],
        out_specs=[vmem] * count,
        compiler_params=pltpu.CompilerParams(vmem_limit_bytes=32 * 2**20),
        cost_estimate=pl.CostEstimate(flops=0, bytes_accessed=3 * 2**20, transcendentals=0),
    )(which, value)


def fits(mesh):
    return mesh.shape["ctx"] == 8 and mesh.shape["ch"] == 4


def after(value, *others):
    return lax.optimization_barrier((value, *others))[0]


def special(features, w_in, short_filter, filter_spectrum, out_grad):
    n = lax.axis_size("ctx")
    m = lax.axis_size("ch")
    place = lax.axis_index("ctx")
    column = lax.axis_index("ch")
    rows, depth = features.shape
    total = rows * n
    share = n // m
    pairs = n // 2
    line = place // 2
    odd = place % 2
    block_depth = w_in.shape[0]
    width = w_in.shape[2]
    own = width // n
    sub = own // PARTS
    sections = n.bit_length() - 1
    flips = [(i, i ^ 1) for i in range(n)]
    shifts = [[(i, (i // 2 + s) % pairs * 2 + i % 2) for i in range(n)] for s in range(pairs)]
    up = [(i, i + 2) for i in range(n - 2)]
    down = [(i + 2, i) for i in range(n - 2)]

    def trade(value, bit):
        return lax.ppermute(value, "ch", [(j, j ^ 1 << bit) for j in range(m)])

    up1 = lax.ppermute(features, "ctx", up)
    down1 = lax.ppermute(features, "ctx", down)

    which = (column + jnp.arange(m, dtype=jnp.int32)) % m
    turned = cut(sub, which, w_in.transpose(1, 0, 2))
    pieces = []
    for step, piece in enumerate(turned):
        hops = []
        for i in range(n):
            for j in range(m):
                hops.append((i * m + j, ((j + step) % m * 2 + i % 2) * m + i // 2))
        if step == m - 1:
            piece = after(piece, up1, down1)
        pieces.append(lax.ppermute(piece, BOTH, hops))
    pieces += [lax.ppermute(piece, "ctx", flips) for piece in pieces]

    mirrored = (reverse_bits(place, sections) > n // 2).astype(jnp.int32)
    packed = pack(jnp.stack([mirrored, column]), filter_spectrum, out_grad, n, m)

    up2 = lax.ppermute(up1, "ctx", up)
    down2 = lax.ppermute(down1, "ctx", down)
    up3 = lax.ppermute(after(up2, packed), "ctx", up)
    down3 = lax.ppermute(after(down2, packed), "ctx", down)
    behind = [
        jnp.where(line >= 1, up1, down3),
        jnp.where(line >= 2, up2, down2),
        jnp.where(line >= 3, up3, down1),
    ]
    whole = jnp.zeros((pairs, rows, depth), features.dtype)
    for shift, value in enumerate([features] + behind):
        value = jnp.where(
            odd == 0,
            value,
            jnp.concatenate([value[:, block_depth:], value[:, :block_depth]], axis=1),
        )
        whole = lax.dynamic_update_slice(whole, value[None], ((line - shift) % pairs, 0, 0))
    whole = whole.reshape(pairs * rows, depth)

    count = m // 2
    spot = 3 * 2 * sub
    weights = jnp.zeros((2, PARTS, count, spot, share * block_depth), w_in.dtype)
    for index, piece in enumerate(pieces):
        block, step = divmod(index, m)
        slot = (line - step) % m ^ column
        weights = lax.dynamic_update_slice(
            weights,
            piece.reshape(1, PARTS, 1, spot, block_depth),
            (slot % 2, 0, slot // 2, 0, block * block_depth),
        )

    def multiply(kind, part):
        left = weights[kind, part].reshape(count * spot, share * block_depth)
        result = lax.dot_general(
            left, whole, (((1,), (1,)), ((), ())), preferred_element_type=jnp.float32
        )
        return result.reshape(count, spot, -1)

    def along(value, *others):
        value = value.reshape(pairs, 2, *value.shape[1:])
        found = []
        for shift in range(pairs):
            piece = lax.dynamic_index_in_dim(value, (line - shift) % pairs, 0, keepdims=False)
            if shift:
                back = [(i, (i // 2 - shift) % pairs * 2 + i % 2) for i in range(n)]
                piece = lax.ppermute(after(piece, *others), "ctx", back)
            found.append(piece)
        found = jnp.stack(found)
        mine = lax.dynamic_index_in_dim(found, odd, 1, keepdims=False)
        give = lax.dynamic_index_in_dim(found, 1 - odd, 1, keepdims=False)
        return mine, lax.ppermute(give, "ctx", flips)

    mine, other = along(packed[:, 0], up3, down3, *pieces[:m])
    response = jnp.concatenate([mine, other]).reshape(n, rows // own, own, -1)
    order = jnp.asarray(ORDER, jnp.int32)
    places = (order % 2 ^ odd) * pairs + (order // 2 - line) % pairs
    places = jnp.concatenate([odd.reshape(1), places])

    taps = lax.dynamic_slice_in_dim(short_filter, place * own, own, 2)
    taps = taps.reshape(3, 3, PARTS, sub).transpose(2, 0, 1, 3).reshape(PARTS, 3, 3 * sub, 1)
    sends = [multiply(1, part) for part in range(PARTS)]
    keeps = [multiply(0, part) for part in range(PARTS)]
    gots = [trade(send, 0) for send in sends]
    onwards = [(keep[1] + got[1]).astype(jnp.bfloat16) for keep, got in zip(keeps, gots)]
    across = [trade(onward, 1) for onward in onwards]
    gated = []
    for part in range(PARTS):
        projected = keeps[part][0] + gots[part][0] + across[part].astype(jnp.float32)
        projected = projected.astype(jnp.bfloat16).reshape(2, 3 * sub, total // 2)
        mine = lax.dynamic_index_in_dim(projected, odd, 0, keepdims=False)
        give = lax.dynamic_index_in_dim(projected, 1 - odd, 0, keepdims=False)
        other = lax.ppermute(give, "ctx", flips)
        gated.append(
            convolve(
                places, mine, other, taps[part],
                response[:, :, part * sub : (part + 1) * sub],
            )
        )

    mine, other = along(packed[:, 1], *onwards)
    low, high = jnp.where(odd == 0, mine, other), jnp.where(odd == 0, other, mine)
    grads = jnp.stack([low, high], axis=1)
    grads = lax.dynamic_slice_in_dim(
        jnp.concatenate([grads, grads]), (pairs - line) % pairs, pairs, 0
    )
    grads = grads.reshape(total, grads.shape[3])
    for bit in (1, 0):
        other = trade(grads, bit)
        low = column >> bit & 1 == 0
        if bit == 1:
            grads = jnp.stack([jnp.where(low, grads, other), jnp.where(low, other, grads)])
        else:
            low, high = jnp.where(low, grads, other), jnp.where(low, other, grads)
            grads = jnp.concatenate([low[0], high[0], low[1], high[1]], axis=1)

    every = jnp.zeros((pairs, 2, PARTS, sub, total), jnp.bfloat16)
    for part in range(PARTS):
        near = [gated[part]]
        near += [lax.ppermute(gated[part], "ctx", shifts[s]) for s in range(1, pairs)]
        near = jnp.stack(near)
        other = lax.ppermute(near, "ctx", flips)
        low = jnp.where(odd == 0, near, other)
        high = jnp.where(odd == 0, other, near)
        for shift in range(pairs):
            every = lax.dynamic_update_slice(
                every,
                jnp.stack([low[shift], high[shift]])[None, :, None],
                ((line - shift) % pairs, 0, part, 0, 0),
            )
    every = every.reshape(width, total)
    w_out_grad = lax.dot_general(
        grads, every, (((0,), (1,)), ((), ())), preferred_element_type=jnp.float32
    )
    out = lax.dynamic_slice_in_dim(every, place * rows, rows, 1).T
    return (out, w_out_grad)


def solution(mesh):
    in_specs = (
        P("ctx", "ch"),
        P("ctx", None, "ch"),
        P(None, None, "ch"),
        P(None, "ctx", "ch"),
        P("ctx", None),
    )
    out_specs = (P("ctx", "ch"), P("ctx", "ch"))
    on_device = special if fits(mesh) else general
    return jax.shard_map(
        on_device, mesh=mesh, in_specs=in_specs, out_specs=out_specs, check_vma=False
    )
```

```python
import functools
import math

import jax
import jax.numpy as jnp
import numpy as np
from jax import lax
from jax.experimental import pallas as pl
from jax.experimental.pallas import tpu as pltpu
from jax.sharding import PartitionSpec as P

TWO_PI = 2.0 * math.pi
BOTH = ("ctx", "ch")
ORDER = (0, 4, 2, 6, 1, 5, 3, 7)


def product(spec, left, right):
    return jnp.einsum(
        spec, left, right, precision=lax.Precision.HIGHEST, preferred_element_type=jnp.float32
    )


def reverse_bits(values, count):
    result = jnp.zeros_like(values)
    for level in range(count):
        result = result | (values >> level & 1) << count - 1 - level
    return result


def phase_tables(phase, period):
    angle = TWO_PI / period * phase.astype(jnp.float32)
    return (jnp.cos(angle), jnp.sin(angle))


def gather_pairs(value, n, place):
    pairs = n // 2
    odd = place % 2
    near = [value]
    for shift in range(1, pairs):
        hops = [(i, (i // 2 + shift) % pairs * 2 + i % 2) for i in range(n)]
        near.append(lax.ppermute(value, "ctx", hops))
    flips = [(i, i ^ 1) for i in range(n)]
    found = []
    for shift in range(pairs):
        other = lax.ppermute(near[shift], "ctx", flips)
        low = jnp.where(odd == 0, near[shift], other)
        high = jnp.where(odd == 0, other, near[shift])
        found.append(((place // 2 - shift) % pairs, low, high))
    return found


def general(features, w_in, short_filter, filter_spectrum, out_grad):
    n = lax.axis_size("ctx")
    m = lax.axis_size("ch")
    place = lax.axis_index("ctx")
    column = lax.axis_index("ch")
    rows, depth = features.shape
    total = rows * n
    share = n // m
    block_depth = w_in.shape[0]
    width = w_in.shape[2]
    own = width // n
    sections = n.bit_length() - 1

    whole = jnp.zeros((n // 2, 2, rows, depth), features.dtype)
    for index, low, high in gather_pairs(features, n, place):
        whole = lax.dynamic_update_slice(whole, jnp.stack([low, high])[None], (index, 0, 0, 0))
    whole = whole.reshape(total, depth)

    turned = w_in.reshape(block_depth, 3, n, own).transpose(2, 1, 3, 0)
    sender = place % share * m + column
    weights = jnp.zeros((n, 3, own, block_depth), w_in.dtype)
    for step in range(n):
        hops = []
        for i in range(n):
            for j in range(m):
                hops.append((i * m + j, (i % share * m + j + step) % n * m + i // share))
        piece = lax.dynamic_index_in_dim(turned, (sender + step) % n, 0)
        piece = lax.ppermute(piece, BOTH, hops)
        weights = lax.dynamic_update_slice(weights, piece, ((place - step) % n, 0, 0, 0))
    weights = weights.reshape(share, m * 3 * own, block_depth).transpose(1, 0, 2)
    weights = weights.reshape(m * 3 * own, depth)

    partial = lax.dot_general(
        weights, whole, (((1,), (1,)), ((), ())), preferred_element_type=jnp.float32
    )
    partial = partial.reshape(m, 3 * own, total)
    bits = m.bit_length() - 1
    for bit in range(bits):
        mine = column >> bit & 1
        halves = partial.reshape(-1, 2, 3 * own, total)
        keep = lax.dynamic_index_in_dim(halves, mine, 1, keepdims=False)
        send = lax.dynamic_index_in_dim(halves, 1 - mine, 1, keepdims=False)
        if bit == bits - 1:
            send = send.astype(jnp.bfloat16)
        flips = [(j, j ^ 1 << bit) for j in range(m)]
        partial = keep + lax.ppermute(send, "ch", flips).astype(jnp.float32)
    projected = partial.reshape(3, own, total).astype(jnp.bfloat16).astype(jnp.float32)

    taps = lax.dynamic_slice_in_dim(short_filter, place * own, own, 2)[:, :, :, None]
    padded = jnp.pad(projected, ((0, 0), (0, 0), (2, 0)))
    mixed = (
        taps[0] * projected + taps[1] * padded[:, :, 1 : total + 1] + taps[2] * padded[:, :, :total]
    )
    query = mixed[0]
    signal = (mixed[1] * mixed[2]).reshape(own, n, rows)

    response = lax.all_to_all(
        filter_spectrum.reshape(2, rows, n, own).transpose(2, 3, 0, 1),
        "ctx", split_axis=0, concat_axis=0, tiled=True,
    )
    grid = lax.broadcasted_iota(jnp.int32, (rows, rows), 0) * lax.broadcasted_iota(
        jnp.int32, (rows, rows), 1
    )
    local_cos, local_sin = phase_tables(grid % rows, rows)
    order = reverse_bits(lax.broadcasted_iota(jnp.int32, (n, 1), 0), sections)
    across = order * lax.broadcasted_iota(jnp.int32, (1, n), 1)
    across_cos, across_sin = phase_tables(across % n, n)
    turn = order * lax.broadcasted_iota(jnp.int32, (1, rows), 1)
    turn_cos, turn_sin = phase_tables(turn % total, total)
    turn_cos, turn_sin = turn_cos[:, None], turn_sin[:, None]
    real = product("rn,cnt->rct", across_cos, signal)
    imag = -product("rn,cnt->rct", across_sin, signal)
    real, imag = real * turn_cos + imag * turn_sin, imag * turn_cos - real * turn_sin
    spec_real = product("rct,tq->rcq", real, local_cos) + product("rct,tq->rcq", imag, local_sin)
    spec_imag = product("rct,tq->rcq", imag, local_cos) - product("rct,tq->rcq", real, local_sin)
    res_real, res_imag = response[:, :, 0], response[:, :, 1]
    prod_real = spec_real * res_real - spec_imag * res_imag
    prod_imag = spec_real * res_imag + spec_imag * res_real
    back_real = product("rcq,qt->rct", prod_real, local_cos) - product(
        "rcq,qt->rct", prod_imag, local_sin
    )
    back_imag = product("rcq,qt->rct", prod_imag, local_cos) + product(
        "rcq,qt->rct", prod_real, local_sin
    )
    back_real, back_imag = (
        back_real * turn_cos - back_imag * turn_sin,
        back_imag * turn_cos + back_real * turn_sin,
    )
    convolved = (
        product("rn,rct->cnt", across_cos, back_real)
        - product("rn,rct->cnt", across_sin, back_imag)
    ) / total
    gated = (query * convolved.reshape(own, total)).astype(jnp.bfloat16)

    out_rows = out_grad.shape[1] // n
    part = out_rows // m
    mine = lax.dynamic_index_in_dim(
        out_grad.reshape(rows, n, m, part), column, 2, keepdims=False
    )
    mine = lax.all_to_all(mine, "ctx", split_axis=1, concat_axis=0, tiled=True)
    grads = lax.all_gather(mine.reshape(total, part), "ch", axis=1, tiled=True)

    every = jnp.zeros((n // 2, 2, own, total), jnp.bfloat16)
    for index, low, high in gather_pairs(gated, n, place):
        every = lax.dynamic_update_slice(every, jnp.stack([low, high])[None], (index, 0, 0, 0))
    every = every.reshape(width, total)
    w_out_grad = lax.dot_general(
        grads, every, (((0,), (1,)), ((), ())), preferred_element_type=jnp.float32
    )
    out = lax.dynamic_slice_in_dim(every, place * rows, rows, 1).T
    return (out, w_out_grad)


def exact(left, right):
    return jnp.dot(left, right, precision=lax.Precision.HIGHEST, preferred_element_type=jnp.float32)

def tables(rows, lanes):
    grid = np.arange(rows)[:, None] * np.arange(rows)[None, :] % rows
    angle = 2.0 * math.pi / rows * grid
    table = np.zeros((rows, 2 * lanes), np.float32)
    table[:, :rows] = np.cos(angle)
    table[:, lanes : lanes + rows] = np.sin(angle)
    turn = 2.0 * math.pi / (8 * rows) * (np.arange(5)[:, None] * np.arange(rows)[None, :])
    return table, np.stack([np.cos(turn), np.sin(turn)]).astype(np.float32)

def convolve_kernel(odd_ref, mine_ref, other_ref, taps_ref, response_ref, table_ref, turn_ref, out_ref):
    own, total = out_ref.shape
    rows = total // 8
    lanes = table_ref.shape[1] // 2
    mine, other = mine_ref[...].astype(jnp.float32), other_ref[...].astype(jnp.float32)
    even, uneven = jnp.where(odd_ref[0] == 0, mine, other), jnp.where(odd_ref[0] == 0, other, mine)
    slabs = []
    for spot in range(4):
        slabs += [even[:, rows * spot : rows * (spot + 1)], uneven[:, rows * spot : rows * (spot + 1)]]
    projected = jnp.concatenate(slabs, axis=1)
    lane = lax.broadcasted_iota(jnp.int32, projected.shape, 1)
    mixed = taps_ref[0] * projected
    for back in (1, 2):
        moved = jnp.where(lane < back, 0.0, pltpu.roll(projected, back, 1))
        mixed += taps_ref[back] * moved
    query = mixed[:own]
    signal = mixed[own : 2 * own] * mixed[2 * own :]
    a = [signal[:, rows * i : rows * (i + 1)] for i in range(8)]
    half = math.sqrt(0.5)
    s04, d04, s26, d26 = a[0] + a[4], a[0] - a[4], a[2] + a[6], a[2] - a[6]
    s15, d15, s37, d37 = a[1] + a[5], a[1] - a[5], a[3] + a[7], a[3] - a[7]
    e, f = s04 + s26, s15 + s37
    g, h = half * (d15 - d37), half * (d15 + d37)
    real = [e + f, d04 + g, s04 - s26, d04 - g, e - f]
    imag = [None, -(d26 + h), s37 - s15, d26 - h, None]
    ins = [real[0]]
    for r in range(1, 5):
        cos, sin = turn_ref[0, r : r + 1], turn_ref[1, r : r + 1]
        if imag[r] is None:
            ins += [real[r] * cos, -real[r] * sin]
        else:
            ins += [real[r] * cos + imag[r] * sin, imag[r] * cos - real[r] * sin]
    spectrum = exact(jnp.concatenate(ins, axis=0), table_ref[...])
    response = [
        jnp.concatenate([response_ref[odd_ref[1 + r], i] for i in range(response_ref.shape[1])], axis=1)
        for r in range(8)
    ]
    response = [value.astype(jnp.float32) for value in response]
    outs = []
    for r in range(5):
        if r == 0:
            first = spectrum[:own]
            spec_real, spec_imag = first[:, :rows], -first[:, lanes : lanes + rows]
        else:
            first = spectrum[(2 * r - 1) * own : 2 * r * own]
            second = spectrum[2 * r * own : (2 * r + 1) * own]
            spec_real = first[:, :rows] + second[:, lanes : lanes + rows]
            spec_imag = second[:, :rows] - first[:, lanes : lanes + rows]
        own_class = response[r]
        res_real, res_imag = own_class[:, :rows], own_class[:, rows:]
        if r in (1, 2, 3):
            mirrored = response[8 - r]
            res_real = 0.5 * (res_real + mirrored[:, :rows])
            res_imag = 0.5 * (res_imag - mirrored[:, rows:])
        outs += [spec_real * res_real - spec_imag * res_imag, spec_real * res_imag + spec_imag * res_real]
    back = exact(jnp.concatenate(outs, axis=0), table_ref[...])
    u_real, u_imag = [], []
    for r in range(5):
        first = back[2 * r * own : (2 * r + 1) * own]
        second = back[(2 * r + 1) * own : (2 * r + 2) * own]
        v_real = first[:, :rows] - second[:, lanes : lanes + rows]
        if r == 0:
            u_real.append(v_real)
            u_imag.append(None)
            continue
        v_imag = second[:, :rows] + first[:, lanes : lanes + rows]
        cos, sin = turn_ref[0, r : r + 1], turn_ref[1, r : r + 1]
        u_real.append(v_real * cos - v_imag * sin)
        u_imag.append(None if r == 4 else v_imag * cos + v_real * sin)
    p, q = u_real[0] + u_real[4], u_real[0] - u_real[4]
    r13, i13 = u_real[1] + u_real[3], u_imag[1] - u_imag[3]
    dr, di = half * (u_real[1] - u_real[3]), half * (u_imag[1] + u_imag[3])
    two = 2.0
    r2, i2 = u_real[2], u_imag[2]
    y = [p + two * (r13 + r2), q + two * (dr - di - i2), p - two * (i13 + r2), q + two * (i2 - dr - di),
         p + two * (r2 - r13), q + two * (di - dr - i2), p + two * (i13 - r2), q + two * (dr + di + i2)]
    scale = 1.0 / total
    convolved = jnp.concatenate(y, axis=1) * scale
    out_ref[...] = (query * convolved).astype(jnp.bfloat16)

def convolve(odd, mine, other, taps, response):
    total = 2 * mine.shape[1]
    own = mine.shape[0] // 3
    rows = total // 8
    table, turn = tables(rows, -(-rows // 128) * 128)
    return pl.pallas_call(convolve_kernel, out_shape=jax.ShapeDtypeStruct((own, total), jnp.bfloat16),
        in_specs=[pl.BlockSpec(memory_space=pltpu.SMEM)] + [pl.BlockSpec(memory_space=pltpu.VMEM)] * 6,
        compiler_params=pltpu.CompilerParams(vmem_limit_bytes=48*2**20),
        cost_estimate=pl.CostEstimate(flops=10**9, bytes_accessed=4*10**6, transcendentals=0),
    )(odd, mine, other, taps, response, jnp.asarray(table), jnp.asarray(turn))


PARTS = 2


def pack_kernel(flag_ref, value_ref, grad_ref, out_ref):
    rows = value_ref.shape[1]
    n, _, count, lanes = out_ref.shape
    own = value_ref.shape[2] // n
    down = lax.broadcasted_iota(jnp.int32, (rows, rows), 0)
    along = lax.broadcasted_iota(jnp.int32, (rows, rows), 1)
    target = jnp.where(flag_ref[0] == 1, rows - 1 - down, down)
    swap = (along == target).astype(jnp.bfloat16)
    turned = [
        lax.dot_general(
            value_ref[part].astype(jnp.bfloat16),
            swap,
            (((0,), (0,)), ((), ())),
            preferred_element_type=jnp.float32,
        ).astype(jnp.bfloat16)
        for part in range(2)
    ]
    turned = jnp.concatenate(turned, axis=1)
    step = grad_ref.shape[1] // n
    for place in range(n):
        for chunk in range(count // own):
            out_ref[place, 0, own * chunk : own * (chunk + 1)] = turned[
                own * place : own * (place + 1), lanes * chunk : lanes * (chunk + 1)
            ]
        start = pl.multiple_of(place * step + flag_ref[1] * lanes, lanes)
        out_ref[place, 1] = grad_ref[:, pl.ds(start, lanes)]


def pack(flags, value, grad, n, m):
    rows = grad.shape[0]
    lanes = grad.shape[1] // (n * m)
    vmem = pl.BlockSpec(memory_space=pltpu.VMEM)
    return pl.pallas_call(
        pack_kernel,
        out_shape=jax.ShapeDtypeStruct((n, 2, rows, lanes), jnp.bfloat16),
        in_specs=[pl.BlockSpec(memory_space=pltpu.SMEM), vmem, vmem],
        out_specs=vmem,
        compiler_params=pltpu.CompilerParams(vmem_limit_bytes=32 * 2**20),
        cost_estimate=pl.CostEstimate(flops=10**8, bytes_accessed=4 * 2**20, transcendentals=0),
    )(flags, value, grad)


def cut_kernel(step, which_ref, value_ref, *outs):
    kinds, _, width = value_ref.shape
    size = width // len(outs)
    for index, out_ref in enumerate(outs):
        start = pl.multiple_of(which_ref[index] * size, size)
        for kind in range(kinds):
            piece = value_ref[kind, :, pl.ds(start, size)].T
            for group in range(size // step):
                place = group % PARTS * 2 + group // PARTS
                first = (place * kinds + kind) * step
                out_ref[first : first + step] = piece[group * step : (group + 1) * step]


def cut(step, which, value):
    kinds, deep, width = value.shape
    vmem = pl.BlockSpec(memory_space=pltpu.VMEM)
    count = which.shape[0]
    out = jax.ShapeDtypeStruct((kinds * width // count, deep), value.dtype)
    return pl.pallas_call(
        functools.partial(cut_kernel, step),
        out_shape=[out] * count,
        in_specs=[pl.BlockSpec(memory_space=pltpu.SMEM), vmem],
        out_specs=[vmem] * count,
        compiler_params=pltpu.CompilerParams(vmem_limit_bytes=32 * 2**20),
        cost_estimate=pl.CostEstimate(flops=0, bytes_accessed=3 * 2**20, transcendentals=0),
    )(which, value)


def fits(mesh):
    return mesh.shape["ctx"] == 8 and mesh.shape["ch"] == 4


def after(value, *others):
    return lax.optimization_barrier((value, *others))[0]


def special(features, w_in, short_filter, filter_spectrum, out_grad):
    n = lax.axis_size("ctx")
    m = lax.axis_size("ch")
    place = lax.axis_index("ctx")
    column = lax.axis_index("ch")
    rows, depth = features.shape
    total = rows * n
    share = n // m
    pairs = n // 2
    line = place // 2
    odd = place % 2
    block_depth = w_in.shape[0]
    width = w_in.shape[2]
    own = width // n
    sub = own // PARTS
    sections = n.bit_length() - 1
    flips = [(i, i ^ 1) for i in range(n)]
    shifts = [[(i, (i // 2 + s) % pairs * 2 + i % 2) for i in range(n)] for s in range(pairs)]
    up = [(i, i + 2) for i in range(n - 2)]
    down = [(i + 2, i) for i in range(n - 2)]

    def trade(value, bit):
        return lax.ppermute(value, "ch", [(j, j ^ 1 << bit) for j in range(m)])

    up1 = lax.ppermute(features, "ctx", up)
    down1 = lax.ppermute(features, "ctx", down)

    which = (column + jnp.arange(m, dtype=jnp.int32)) % m
    turned = cut(sub, which, w_in.transpose(1, 0, 2))
    pieces = []
    for step, piece in enumerate(turned):
        hops = []
        for i in range(n):
            for j in range(m):
                hops.append((i * m + j, ((j + step) % m * 2 + i % 2) * m + i // 2))
        if step == m - 1:
            piece = after(piece, up1, down1)
        pieces.append(lax.ppermute(piece, BOTH, hops))
    pieces += [lax.ppermute(piece, "ctx", flips) for piece in pieces]

    mirrored = (reverse_bits(place, sections) > n // 2).astype(jnp.int32)
    packed = pack(jnp.stack([mirrored, column]), filter_spectrum, out_grad, n, m)

    up2 = lax.ppermute(up1, "ctx", up)
    down2 = lax.ppermute(down1, "ctx", down)
    up3 = lax.ppermute(after(up2, packed), "ctx", up)
    down3 = lax.ppermute(after(down2, packed), "ctx", down)
    behind = [
        jnp.where(line >= 1, up1, down3),
        jnp.where(line >= 2, up2, down2),
        jnp.where(line >= 3, up3, down1),
    ]
    def along(value, *others):
        value = value.reshape(pairs, 2, *value.shape[1:])
        found = []
        for shift in range(pairs):
            piece = lax.dynamic_index_in_dim(value, (line - shift) % pairs, 0, keepdims=False)
            if shift:
                back = [(i, (i // 2 - shift) % pairs * 2 + i % 2) for i in range(n)]
                piece = lax.ppermute(after(piece, *others), "ctx", back)
            found.append(piece)
        return found

    filters = along(packed[:, 0], up3, down3, *pieces[:m])

    whole = jnp.zeros((pairs, rows, depth), features.dtype)
    for shift, value in enumerate([features] + behind):
        value = jnp.where(
            odd == 0,
            value,
            jnp.concatenate([value[:, block_depth:], value[:, :block_depth]], axis=1),
        )
        whole = lax.dynamic_update_slice(whole, value[None], ((line - shift) % pairs, 0, 0))
    whole = after(whole.reshape(pairs * rows, depth), *filters)

    count = m // 2
    spot = 3 * 2 * sub
    weights = jnp.zeros((2, PARTS, count, spot, share * block_depth), w_in.dtype)
    for index, piece in enumerate(pieces):
        block, step = divmod(index, m)
        slot = (line - step) % m ^ column
        weights = lax.dynamic_update_slice(
            weights,
            piece.reshape(1, PARTS, 1, spot, block_depth),
            (slot % 2, 0, slot // 2, 0, block * block_depth),
        )

    def multiply(kind, part):
        left = weights[kind, part].reshape(count * spot, share * block_depth)
        result = lax.dot_general(
            left, whole, (((1,), (1,)), ((), ())), preferred_element_type=jnp.float32
        )
        return result.reshape(count, spot, -1)

    def beside(found, *others):
        found = jnp.stack([after(value, *others) for value in found])
        mine = lax.dynamic_index_in_dim(found, odd, 1, keepdims=False)
        give = lax.dynamic_index_in_dim(found, 1 - odd, 1, keepdims=False)
        return mine, lax.ppermute(give, "ctx", flips)

    order = jnp.asarray(ORDER, jnp.int32)
    places = (order % 2 ^ odd) * pairs + (order // 2 - line) % pairs
    places = jnp.concatenate([odd.reshape(1), places])

    taps = lax.dynamic_slice_in_dim(short_filter, place * own, own, 2)
    taps = taps.reshape(3, 3, PARTS, sub).transpose(2, 0, 1, 3).reshape(PARTS, 3, 3 * sub, 1)
    sends = [multiply(1, part) for part in range(PARTS)]
    keeps = [multiply(0, part) for part in range(PARTS)]
    gots = [trade(send, 0) for send in sends]
    onwards = [(keep[1] + got[1]).astype(jnp.bfloat16) for keep, got in zip(keeps, gots)]
    across = [trade(onward, 1) for onward in onwards]
    mine, other = beside(filters, onwards[0])
    response = jnp.concatenate([mine, other]).reshape(n, rows // own, own, -1)
    gated = []
    crossed = []
    gives = []
    for part in range(PARTS):
        projected = keeps[part][0] + gots[part][0] + after(across[part], *crossed).astype(jnp.float32)
        projected = projected.astype(jnp.bfloat16).reshape(2, 3 * sub, total // 2)
        mine = lax.dynamic_index_in_dim(projected, odd, 0, keepdims=False)
        give = lax.dynamic_index_in_dim(projected, 1 - odd, 0, keepdims=False)
        other = lax.ppermute(give, "ctx", flips)
        crossed.append(other)
        gives.append(give)
        gated.append(
            convolve(
                places, mine, other, taps[part],
                response[:, :, part * sub : (part + 1) * sub],
            )
        )

    mine, other = beside(along(packed[:, 1], *onwards), crossed[0], *gives)
    gates = [crossed, [other]]
    low, high = jnp.where(odd == 0, mine, other), jnp.where(odd == 0, other, mine)
    grads = jnp.stack([low, high], axis=1)
    grads = lax.dynamic_slice_in_dim(
        jnp.concatenate([grads, grads]), (pairs - line) % pairs, pairs, 0
    )
    grads = grads.reshape(total, grads.shape[3])
    for bit in (1, 0):
        other = trade(grads, bit)
        low = column >> bit & 1 == 0
        if bit == 1:
            grads = jnp.stack([jnp.where(low, grads, other), jnp.where(low, other, grads)])
        else:
            low, high = jnp.where(low, grads, other), jnp.where(low, other, grads)
            grads = jnp.concatenate([low[0], high[0], low[1], high[1]], axis=1)

    every = jnp.zeros((pairs, 2, PARTS, sub, total), jnp.bfloat16)
    for part in range(PARTS):
        near = [gated[part]]
        near += [lax.ppermute(gated[part], "ctx", shifts[s]) for s in range(1, pairs)]
        near = [after(value, *gates[part]) for value in near]
        near = jnp.stack(near)
        other = lax.ppermute(near, "ctx", flips)
        low = jnp.where(odd == 0, near, other)
        high = jnp.where(odd == 0, other, near)
        for shift in range(pairs):
            every = lax.dynamic_update_slice(
                every,
                jnp.stack([low[shift], high[shift]])[None, :, None],
                ((line - shift) % pairs, 0, part, 0, 0),
            )
    every = every.reshape(width, total)
    w_out_grad = lax.dot_general(
        grads, every, (((0,), (1,)), ((), ())), preferred_element_type=jnp.float32
    )
    out = lax.dynamic_slice_in_dim(every, place * rows, rows, 1).T
    return (out, w_out_grad)


def solution(mesh):
    in_specs = (
        P("ctx", "ch"),
        P("ctx", None, "ch"),
        P(None, None, "ch"),
        P(None, "ctx", "ch"),
        P("ctx", None),
    )
    out_specs = (P("ctx", "ch"), P("ctx", "ch"))
    on_device = special if fits(mesh) else general
    return jax.shard_map(
        on_device, mesh=mesh, in_specs=in_specs, out_specs=out_specs, check_vma=False
    )
```

```python
import functools
import math

import jax
import jax.numpy as jnp
import numpy as np
from jax import lax
from jax.experimental import pallas as pl
from jax.experimental.pallas import tpu as pltpu
from jax.sharding import PartitionSpec as P

TWO_PI = 2.0 * math.pi
BOTH = ("ctx", "ch")
ORDER = (0, 4, 2, 6, 1, 5, 3, 7)


def product(spec, left, right):
    return jnp.einsum(
        spec, left, right, precision=lax.Precision.HIGHEST, preferred_element_type=jnp.float32
    )


def reverse_bits(values, count):
    result = jnp.zeros_like(values)
    for level in range(count):
        result = result | (values >> level & 1) << count - 1 - level
    return result


def phase_tables(phase, period):
    angle = TWO_PI / period * phase.astype(jnp.float32)
    return (jnp.cos(angle), jnp.sin(angle))


def gather_pairs(value, n, place):
    pairs = n // 2
    odd = place % 2
    near = [value]
    for shift in range(1, pairs):
        hops = [(i, (i // 2 + shift) % pairs * 2 + i % 2) for i in range(n)]
        near.append(lax.ppermute(value, "ctx", hops))
    flips = [(i, i ^ 1) for i in range(n)]
    found = []
    for shift in range(pairs):
        other = lax.ppermute(near[shift], "ctx", flips)
        low = jnp.where(odd == 0, near[shift], other)
        high = jnp.where(odd == 0, other, near[shift])
        found.append(((place // 2 - shift) % pairs, low, high))
    return found


def general(features, w_in, short_filter, filter_spectrum, out_grad):
    n = lax.axis_size("ctx")
    m = lax.axis_size("ch")
    place = lax.axis_index("ctx")
    column = lax.axis_index("ch")
    rows, depth = features.shape
    total = rows * n
    share = n // m
    block_depth = w_in.shape[0]
    width = w_in.shape[2]
    own = width // n
    sections = n.bit_length() - 1

    whole = jnp.zeros((n // 2, 2, rows, depth), features.dtype)
    for index, low, high in gather_pairs(features, n, place):
        whole = lax.dynamic_update_slice(whole, jnp.stack([low, high])[None], (index, 0, 0, 0))
    whole = whole.reshape(total, depth)

    turned = w_in.reshape(block_depth, 3, n, own).transpose(2, 1, 3, 0)
    sender = place % share * m + column
    weights = jnp.zeros((n, 3, own, block_depth), w_in.dtype)
    for step in range(n):
        hops = []
        for i in range(n):
            for j in range(m):
                hops.append((i * m + j, (i % share * m + j + step) % n * m + i // share))
        piece = lax.dynamic_index_in_dim(turned, (sender + step) % n, 0)
        piece = lax.ppermute(piece, BOTH, hops)
        weights = lax.dynamic_update_slice(weights, piece, ((place - step) % n, 0, 0, 0))
    weights = weights.reshape(share, m * 3 * own, block_depth).transpose(1, 0, 2)
    weights = weights.reshape(m * 3 * own, depth)

    partial = lax.dot_general(
        weights, whole, (((1,), (1,)), ((), ())), preferred_element_type=jnp.float32
    )
    partial = partial.reshape(m, 3 * own, total)
    bits = m.bit_length() - 1
    for bit in range(bits):
        mine = column >> bit & 1
        halves = partial.reshape(-1, 2, 3 * own, total)
        keep = lax.dynamic_index_in_dim(halves, mine, 1, keepdims=False)
        send = lax.dynamic_index_in_dim(halves, 1 - mine, 1, keepdims=False)
        if bit == bits - 1:
            send = send.astype(jnp.bfloat16)
        flips = [(j, j ^ 1 << bit) for j in range(m)]
        partial = keep + lax.ppermute(send, "ch", flips).astype(jnp.float32)
    projected = partial.reshape(3, own, total).astype(jnp.bfloat16).astype(jnp.float32)

    taps = lax.dynamic_slice_in_dim(short_filter, place * own, own, 2)[:, :, :, None]
    padded = jnp.pad(projected, ((0, 0), (0, 0), (2, 0)))
    mixed = (
        taps[0] * projected + taps[1] * padded[:, :, 1 : total + 1] + taps[2] * padded[:, :, :total]
    )
    query = mixed[0]
    signal = (mixed[1] * mixed[2]).reshape(own, n, rows)

    response = lax.all_to_all(
        filter_spectrum.reshape(2, rows, n, own).transpose(2, 3, 0, 1),
        "ctx", split_axis=0, concat_axis=0, tiled=True,
    )
    grid = lax.broadcasted_iota(jnp.int32, (rows, rows), 0) * lax.broadcasted_iota(
        jnp.int32, (rows, rows), 1
    )
    local_cos, local_sin = phase_tables(grid % rows, rows)
    order = reverse_bits(lax.broadcasted_iota(jnp.int32, (n, 1), 0), sections)
    across = order * lax.broadcasted_iota(jnp.int32, (1, n), 1)
    across_cos, across_sin = phase_tables(across % n, n)
    turn = order * lax.broadcasted_iota(jnp.int32, (1, rows), 1)
    turn_cos, turn_sin = phase_tables(turn % total, total)
    turn_cos, turn_sin = turn_cos[:, None], turn_sin[:, None]
    real = product("rn,cnt->rct", across_cos, signal)
    imag = -product("rn,cnt->rct", across_sin, signal)
    real, imag = real * turn_cos + imag * turn_sin, imag * turn_cos - real * turn_sin
    spec_real = product("rct,tq->rcq", real, local_cos) + product("rct,tq->rcq", imag, local_sin)
    spec_imag = product("rct,tq->rcq", imag, local_cos) - product("rct,tq->rcq", real, local_sin)
    res_real, res_imag = response[:, :, 0], response[:, :, 1]
    prod_real = spec_real * res_real - spec_imag * res_imag
    prod_imag = spec_real * res_imag + spec_imag * res_real
    back_real = product("rcq,qt->rct", prod_real, local_cos) - product(
        "rcq,qt->rct", prod_imag, local_sin
    )
    back_imag = product("rcq,qt->rct", prod_imag, local_cos) + product(
        "rcq,qt->rct", prod_real, local_sin
    )
    back_real, back_imag = (
        back_real * turn_cos - back_imag * turn_sin,
        back_imag * turn_cos + back_real * turn_sin,
    )
    convolved = (
        product("rn,rct->cnt", across_cos, back_real)
        - product("rn,rct->cnt", across_sin, back_imag)
    ) / total
    gated = (query * convolved.reshape(own, total)).astype(jnp.bfloat16)

    out_rows = out_grad.shape[1] // n
    part = out_rows // m
    mine = lax.dynamic_index_in_dim(
        out_grad.reshape(rows, n, m, part), column, 2, keepdims=False
    )
    mine = lax.all_to_all(mine, "ctx", split_axis=1, concat_axis=0, tiled=True)
    grads = lax.all_gather(mine.reshape(total, part), "ch", axis=1, tiled=True)

    every = jnp.zeros((n // 2, 2, own, total), jnp.bfloat16)
    for index, low, high in gather_pairs(gated, n, place):
        every = lax.dynamic_update_slice(every, jnp.stack([low, high])[None], (index, 0, 0, 0))
    every = every.reshape(width, total)
    w_out_grad = lax.dot_general(
        grads, every, (((0,), (1,)), ((), ())), preferred_element_type=jnp.float32
    )
    out = lax.dynamic_slice_in_dim(every, place * rows, rows, 1).T
    return (out, w_out_grad)


def exact(left, right):
    return jnp.dot(left, right, precision=lax.Precision.HIGHEST, preferred_element_type=jnp.float32)

def tables(rows, lanes):
    grid = np.arange(rows)[:, None] * np.arange(rows)[None, :] % rows
    angle = 2.0 * math.pi / rows * grid
    table = np.zeros((rows, 2 * lanes), np.float32)
    table[:, :rows] = np.cos(angle)
    table[:, lanes : lanes + rows] = np.sin(angle)
    turn = 2.0 * math.pi / (8 * rows) * (np.arange(5)[:, None] * np.arange(rows)[None, :])
    return table, np.stack([np.cos(turn), np.sin(turn)]).astype(np.float32)

def convolve_kernel(odd_ref, mine_ref, other_ref, taps_ref, response_ref, table_ref, turn_ref, out_ref):
    own, total = out_ref.shape
    rows = total // 8
    lanes = table_ref.shape[1] // 2
    mine, other = mine_ref[...].astype(jnp.float32), other_ref[...].astype(jnp.float32)
    even, uneven = jnp.where(odd_ref[0] == 0, mine, other), jnp.where(odd_ref[0] == 0, other, mine)
    slabs = []
    for spot in range(4):
        slabs += [even[:, rows * spot : rows * (spot + 1)], uneven[:, rows * spot : rows * (spot + 1)]]
    projected = jnp.concatenate(slabs, axis=1)
    lane = lax.broadcasted_iota(jnp.int32, projected.shape, 1)
    mixed = taps_ref[0] * projected
    for back in (1, 2):
        moved = jnp.where(lane < back, 0.0, pltpu.roll(projected, back, 1))
        mixed += taps_ref[back] * moved
    query = mixed[:own]
    signal = mixed[own : 2 * own] * mixed[2 * own :]
    a = [signal[:, rows * i : rows * (i + 1)] for i in range(8)]
    half = math.sqrt(0.5)
    s04, d04, s26, d26 = a[0] + a[4], a[0] - a[4], a[2] + a[6], a[2] - a[6]
    s15, d15, s37, d37 = a[1] + a[5], a[1] - a[5], a[3] + a[7], a[3] - a[7]
    e, f = s04 + s26, s15 + s37
    g, h = half * (d15 - d37), half * (d15 + d37)
    real = [e + f, d04 + g, s04 - s26, d04 - g, e - f]
    imag = [None, -(d26 + h), s37 - s15, d26 - h, None]
    ins = [real[0]]
    for r in range(1, 5):
        cos, sin = turn_ref[0, r : r + 1], turn_ref[1, r : r + 1]
        if imag[r] is None:
            ins += [real[r] * cos, -real[r] * sin]
        else:
            ins += [real[r] * cos + imag[r] * sin, imag[r] * cos - real[r] * sin]
    spectrum = exact(jnp.concatenate(ins, axis=0), table_ref[...])
    response = [
        jnp.concatenate([response_ref[odd_ref[1 + r], i] for i in range(response_ref.shape[1])], axis=1)
        for r in range(8)
    ]
    response = [value.astype(jnp.float32) for value in response]
    outs = []
    for r in range(5):
        if r == 0:
            first = spectrum[:own]
            spec_real, spec_imag = first[:, :rows], -first[:, lanes : lanes + rows]
        else:
            first = spectrum[(2 * r - 1) * own : 2 * r * own]
            second = spectrum[2 * r * own : (2 * r + 1) * own]
            spec_real = first[:, :rows] + second[:, lanes : lanes + rows]
            spec_imag = second[:, :rows] - first[:, lanes : lanes + rows]
        own_class = response[r]
        res_real, res_imag = own_class[:, :rows], own_class[:, rows:]
        if r in (1, 2, 3):
            mirrored = response[8 - r]
            res_real = 0.5 * (res_real + mirrored[:, :rows])
            res_imag = 0.5 * (res_imag - mirrored[:, rows:])
        outs += [spec_real * res_real - spec_imag * res_imag, spec_real * res_imag + spec_imag * res_real]
    back = exact(jnp.concatenate(outs, axis=0), table_ref[...])
    u_real, u_imag = [], []
    for r in range(5):
        first = back[2 * r * own : (2 * r + 1) * own]
        second = back[(2 * r + 1) * own : (2 * r + 2) * own]
        v_real = first[:, :rows] - second[:, lanes : lanes + rows]
        if r == 0:
            u_real.append(v_real)
            u_imag.append(None)
            continue
        v_imag = second[:, :rows] + first[:, lanes : lanes + rows]
        cos, sin = turn_ref[0, r : r + 1], turn_ref[1, r : r + 1]
        u_real.append(v_real * cos - v_imag * sin)
        u_imag.append(None if r == 4 else v_imag * cos + v_real * sin)
    p, q = u_real[0] + u_real[4], u_real[0] - u_real[4]
    r13, i13 = u_real[1] + u_real[3], u_imag[1] - u_imag[3]
    dr, di = half * (u_real[1] - u_real[3]), half * (u_imag[1] + u_imag[3])
    two = 2.0
    r2, i2 = u_real[2], u_imag[2]
    y = [p + two * (r13 + r2), q + two * (dr - di - i2), p - two * (i13 + r2), q + two * (i2 - dr - di),
         p + two * (r2 - r13), q + two * (di - dr - i2), p + two * (i13 - r2), q + two * (dr + di + i2)]
    scale = 1.0 / total
    convolved = jnp.concatenate(y, axis=1) * scale
    out_ref[...] = (query * convolved).astype(jnp.bfloat16)

def convolve(odd, mine, other, taps, response):
    total = 2 * mine.shape[1]
    own = mine.shape[0] // 3
    rows = total // 8
    table, turn = tables(rows, -(-rows // 128) * 128)
    return pl.pallas_call(convolve_kernel, out_shape=jax.ShapeDtypeStruct((own, total), jnp.bfloat16),
        in_specs=[pl.BlockSpec(memory_space=pltpu.SMEM)] + [pl.BlockSpec(memory_space=pltpu.VMEM)] * 6,
        compiler_params=pltpu.CompilerParams(vmem_limit_bytes=48*2**20),
        cost_estimate=pl.CostEstimate(flops=10**9, bytes_accessed=4*10**6, transcendentals=0),
    )(odd, mine, other, taps, response, jnp.asarray(table), jnp.asarray(turn))


PARTS = 2


def pack_kernel(flag_ref, value_ref, grad_ref, out_ref):
    rows = value_ref.shape[1]
    n, _, count, lanes = out_ref.shape
    own = value_ref.shape[2] // n
    down = lax.broadcasted_iota(jnp.int32, (rows, rows), 0)
    along = lax.broadcasted_iota(jnp.int32, (rows, rows), 1)
    target = jnp.where(flag_ref[0] == 1, rows - 1 - down, down)
    swap = (along == target).astype(jnp.bfloat16)
    turned = [
        lax.dot_general(
            value_ref[part].astype(jnp.bfloat16),
            swap,
            (((0,), (0,)), ((), ())),
            preferred_element_type=jnp.float32,
        ).astype(jnp.bfloat16)
        for part in range(2)
    ]
    turned = jnp.concatenate(turned, axis=1)
    step = grad_ref.shape[1] // n
    for place in range(n):
        for chunk in range(count // own):
            out_ref[place, 0, own * chunk : own * (chunk + 1)] = turned[
                own * place : own * (place + 1), lanes * chunk : lanes * (chunk + 1)
            ]
        start = pl.multiple_of(place * step + flag_ref[1] * lanes, lanes)
        out_ref[place, 1] = grad_ref[:, pl.ds(start, lanes)]


def pack(flags, value, grad, n, m):
    rows = grad.shape[0]
    lanes = grad.shape[1] // (n * m)
    vmem = pl.BlockSpec(memory_space=pltpu.VMEM)
    return pl.pallas_call(
        pack_kernel,
        out_shape=jax.ShapeDtypeStruct((n, 2, rows, lanes), jnp.bfloat16),
        in_specs=[pl.BlockSpec(memory_space=pltpu.SMEM), vmem, vmem],
        out_specs=vmem,
        compiler_params=pltpu.CompilerParams(vmem_limit_bytes=32 * 2**20),
        cost_estimate=pl.CostEstimate(flops=10**8, bytes_accessed=4 * 2**20, transcendentals=0),
    )(flags, value, grad)


def cut_kernel(step, which_ref, value_ref, *outs):
    kinds, _, width = value_ref.shape
    size = width // len(outs)
    for index, out_ref in enumerate(outs):
        start = pl.multiple_of(which_ref[index] * size, size)
        for kind in range(kinds):
            piece = value_ref[kind, :, pl.ds(start, size)].T
            for group in range(size // step):
                place = group % PARTS * 2 + group // PARTS
                first = (place * kinds + kind) * step
                out_ref[first : first + step] = piece[group * step : (group + 1) * step]


def cut(step, which, value):
    kinds, deep, width = value.shape
    vmem = pl.BlockSpec(memory_space=pltpu.VMEM)
    count = which.shape[0]
    out = jax.ShapeDtypeStruct((kinds * width // count, deep), value.dtype)
    return pl.pallas_call(
        functools.partial(cut_kernel, step),
        out_shape=[out] * count,
        in_specs=[pl.BlockSpec(memory_space=pltpu.SMEM), vmem],
        out_specs=[vmem] * count,
        compiler_params=pltpu.CompilerParams(vmem_limit_bytes=32 * 2**20),
        cost_estimate=pl.CostEstimate(flops=0, bytes_accessed=3 * 2**20, transcendentals=0),
    )(which, value)


def fits(mesh):
    return mesh.shape["ctx"] == 8 and mesh.shape["ch"] == 4


def after(value, *others):
    return lax.optimization_barrier((value, *others))[0]


def special(features, w_in, short_filter, filter_spectrum, out_grad):
    n = lax.axis_size("ctx")
    m = lax.axis_size("ch")
    place = lax.axis_index("ctx")
    column = lax.axis_index("ch")
    rows, depth = features.shape
    total = rows * n
    share = n // m
    pairs = n // 2
    line = place // 2
    odd = place % 2
    block_depth = w_in.shape[0]
    width = w_in.shape[2]
    own = width // n
    sub = own // PARTS
    sections = n.bit_length() - 1
    flips = [(i, i ^ 1) for i in range(n)]
    shifts = [[(i, (i // 2 + s) % pairs * 2 + i % 2) for i in range(n)] for s in range(pairs)]
    up = [(i, i + 2) for i in range(n - 2)]
    down = [(i + 2, i) for i in range(n - 2)]

    def trade(value, bit):
        return lax.ppermute(value, "ch", [(j, j ^ 1 << bit) for j in range(m)])

    up1 = lax.ppermute(features, "ctx", up)
    down1 = lax.ppermute(features, "ctx", down)

    which = (column + jnp.arange(m, dtype=jnp.int32)) % m
    turned = cut(sub, which, w_in.transpose(1, 0, 2))
    pieces = []
    for step, piece in enumerate(turned):
        hops = []
        for i in range(n):
            for j in range(m):
                hops.append((i * m + j, ((j + step) % m * 2 + i % 2) * m + i // 2))
        if step == m - 1:
            piece = after(piece, up1, down1)
        pieces.append(lax.ppermute(piece, BOTH, hops))
    pieces += [lax.ppermute(piece, "ctx", flips) for piece in pieces]

    mirrored = (reverse_bits(place, sections) > n // 2).astype(jnp.int32)
    packed = pack(jnp.stack([mirrored, column]), filter_spectrum, out_grad, n, m)

    up2 = lax.ppermute(up1, "ctx", up)
    down2 = lax.ppermute(down1, "ctx", down)
    up3 = lax.ppermute(after(up2, packed), "ctx", up)
    down3 = lax.ppermute(after(down2, packed), "ctx", down)
    behind = [
        jnp.where(line >= 1, up1, down3),
        jnp.where(line >= 2, up2, down2),
        jnp.where(line >= 3, up3, down1),
    ]
    def along(value, *others):
        value = value.reshape(pairs, 2, *value.shape[1:])
        found = []
        for shift in range(pairs):
            piece = lax.dynamic_index_in_dim(value, (line - shift) % pairs, 0, keepdims=False)
            if shift:
                back = [(i, (i // 2 - shift) % pairs * 2 + i % 2) for i in range(n)]
                piece = lax.ppermute(after(piece, *others), "ctx", back)
            found.append(piece)
        return found

    filters = along(packed[:, 0], up2, down2)

    whole = jnp.zeros((pairs, rows, depth), features.dtype)
    for shift, value in enumerate([features] + behind):
        value = jnp.where(
            odd == 0,
            value,
            jnp.concatenate([value[:, block_depth:], value[:, :block_depth]], axis=1),
        )
        whole = lax.dynamic_update_slice(whole, value[None], ((line - shift) % pairs, 0, 0))
    whole = whole.reshape(pairs * rows, depth)

    count = m // 2
    spot = 3 * 2 * sub
    weights = jnp.zeros((2, PARTS, count, spot, share * block_depth), w_in.dtype)
    for index, piece in enumerate(pieces):
        block, step = divmod(index, m)
        slot = (line - step) % m ^ column
        weights = lax.dynamic_update_slice(
            weights,
            piece.reshape(1, PARTS, 1, spot, block_depth),
            (slot % 2, 0, slot // 2, 0, block * block_depth),
        )

    def multiply(kind, part):
        left = weights[kind, part].reshape(count * spot, share * block_depth)
        result = lax.dot_general(
            left, whole, (((1,), (1,)), ((), ())), preferred_element_type=jnp.float32
        )
        return result.reshape(count, spot, -1)

    def beside(found, *others):
        found = jnp.stack([after(value, *others) for value in found])
        mine = lax.dynamic_index_in_dim(found, odd, 1, keepdims=False)
        give = lax.dynamic_index_in_dim(found, 1 - odd, 1, keepdims=False)
        return mine, lax.ppermute(give, "ctx", flips)

    order = jnp.asarray(ORDER, jnp.int32)
    places = (order % 2 ^ odd) * pairs + (order // 2 - line) % pairs
    places = jnp.concatenate([odd.reshape(1), places])

    taps = lax.dynamic_slice_in_dim(short_filter, place * own, own, 2)
    taps = taps.reshape(3, 3, PARTS, sub).transpose(2, 0, 1, 3).reshape(PARTS, 3, 3 * sub, 1)
    sends = [multiply(1, part) for part in range(PARTS)]
    keeps = [multiply(0, part) for part in range(PARTS)]
    gots = [trade(send, 0) for send in sends]
    onwards = [(keep[1] + got[1]).astype(jnp.bfloat16) for keep, got in zip(keeps, gots)]
    across = [trade(onward, 1) for onward in onwards]
    mine, other = beside(filters, onwards[0])
    response = jnp.concatenate([mine, other]).reshape(n, rows // own, own, -1)
    gated = []
    crossed = []
    gives = []
    for part in range(PARTS):
        projected = keeps[part][0] + gots[part][0] + after(across[part], *crossed).astype(jnp.float32)
        projected = projected.astype(jnp.bfloat16).reshape(2, 3 * sub, total // 2)
        mine = lax.dynamic_index_in_dim(projected, odd, 0, keepdims=False)
        give = lax.dynamic_index_in_dim(projected, 1 - odd, 0, keepdims=False)
        other = lax.ppermute(give, "ctx", flips)
        crossed.append(other)
        gives.append(give)
        gated.append(
            convolve(
                places, mine, other, taps[part],
                response[:, :, part * sub : (part + 1) * sub],
            )
        )

    mine, other = beside(along(packed[:, 1], *onwards), crossed[0], *gives)
    gates = [crossed, [other]]
    low, high = jnp.where(odd == 0, mine, other), jnp.where(odd == 0, other, mine)
    grads = jnp.stack([low, high], axis=1)
    grads = lax.dynamic_slice_in_dim(
        jnp.concatenate([grads, grads]), (pairs - line) % pairs, pairs, 0
    )
    grads = grads.reshape(total, grads.shape[3])
    for bit in (1, 0):
        other = trade(grads, bit)
        low = column >> bit & 1 == 0
        if bit == 1:
            grads = jnp.stack([jnp.where(low, grads, other), jnp.where(low, other, grads)])
        else:
            low, high = jnp.where(low, grads, other), jnp.where(low, other, grads)
            grads = jnp.concatenate([low[0], high[0], low[1], high[1]], axis=1)

    every = jnp.zeros((pairs, 2, PARTS, sub, total), jnp.bfloat16)
    for part in range(PARTS):
        near = [gated[part]]
        near += [lax.ppermute(gated[part], "ctx", shifts[s]) for s in range(1, pairs)]
        near = [after(value, *gates[part]) for value in near]
        near = jnp.stack(near)
        other = lax.ppermute(near, "ctx", flips)
        low = jnp.where(odd == 0, near, other)
        high = jnp.where(odd == 0, other, near)
        for shift in range(pairs):
            every = lax.dynamic_update_slice(
                every,
                jnp.stack([low[shift], high[shift]])[None, :, None],
                ((line - shift) % pairs, 0, part, 0, 0),
            )
    every = every.reshape(width, total)
    w_out_grad = lax.dot_general(
        grads, every, (((0,), (1,)), ((), ())), preferred_element_type=jnp.float32
    )
    out = lax.dynamic_slice_in_dim(every, place * rows, rows, 1).T
    return (out, w_out_grad)


def solution(mesh):
    in_specs = (
        P("ctx", "ch"),
        P("ctx", None, "ch"),
        P(None, None, "ch"),
        P(None, "ctx", "ch"),
        P("ctx", None),
    )
    out_specs = (P("ctx", "ch"), P("ctx", "ch"))
    on_device = special if fits(mesh) else general
    return jax.shard_map(
        on_device, mesh=mesh, in_specs=in_specs, out_specs=out_specs, check_vma=False
    )
```

```python
import functools
import math

import jax
import jax.numpy as jnp
import numpy as np
from jax import lax
from jax.experimental import pallas as pl
from jax.experimental.pallas import tpu as pltpu
from jax.sharding import PartitionSpec as P

TWO_PI = 2.0 * math.pi
BOTH = ("ctx", "ch")
ORDER = (0, 4, 2, 6, 1, 5, 3, 7)


def product(spec, left, right):
    return jnp.einsum(
        spec, left, right, precision=lax.Precision.HIGHEST, preferred_element_type=jnp.float32
    )


def reverse_bits(values, count):
    result = jnp.zeros_like(values)
    for level in range(count):
        result = result | (values >> level & 1) << count - 1 - level
    return result


def phase_tables(phase, period):
    angle = TWO_PI / period * phase.astype(jnp.float32)
    return (jnp.cos(angle), jnp.sin(angle))


def gather_pairs(value, n, place):
    pairs = n // 2
    odd = place % 2
    near = [value]
    for shift in range(1, pairs):
        hops = [(i, (i // 2 + shift) % pairs * 2 + i % 2) for i in range(n)]
        near.append(lax.ppermute(value, "ctx", hops))
    flips = [(i, i ^ 1) for i in range(n)]
    found = []
    for shift in range(pairs):
        other = lax.ppermute(near[shift], "ctx", flips)
        low = jnp.where(odd == 0, near[shift], other)
        high = jnp.where(odd == 0, other, near[shift])
        found.append(((place // 2 - shift) % pairs, low, high))
    return found


def general(features, w_in, short_filter, filter_spectrum, out_grad):
    n = lax.axis_size("ctx")
    m = lax.axis_size("ch")
    place = lax.axis_index("ctx")
    column = lax.axis_index("ch")
    rows, depth = features.shape
    total = rows * n
    share = n // m
    block_depth = w_in.shape[0]
    width = w_in.shape[2]
    own = width // n
    sections = n.bit_length() - 1

    whole = jnp.zeros((n // 2, 2, rows, depth), features.dtype)
    for index, low, high in gather_pairs(features, n, place):
        whole = lax.dynamic_update_slice(whole, jnp.stack([low, high])[None], (index, 0, 0, 0))
    whole = whole.reshape(total, depth)

    turned = w_in.reshape(block_depth, 3, n, own).transpose(2, 1, 3, 0)
    sender = place % share * m + column
    weights = jnp.zeros((n, 3, own, block_depth), w_in.dtype)
    for step in range(n):
        hops = []
        for i in range(n):
            for j in range(m):
                hops.append((i * m + j, (i % share * m + j + step) % n * m + i // share))
        piece = lax.dynamic_index_in_dim(turned, (sender + step) % n, 0)
        piece = lax.ppermute(piece, BOTH, hops)
        weights = lax.dynamic_update_slice(weights, piece, ((place - step) % n, 0, 0, 0))
    weights = weights.reshape(share, m * 3 * own, block_depth).transpose(1, 0, 2)
    weights = weights.reshape(m * 3 * own, depth)

    partial = lax.dot_general(
        weights, whole, (((1,), (1,)), ((), ())), preferred_element_type=jnp.float32
    )
    partial = partial.reshape(m, 3 * own, total)
    bits = m.bit_length() - 1
    for bit in range(bits):
        mine = column >> bit & 1
        halves = partial.reshape(-1, 2, 3 * own, total)
        keep = lax.dynamic_index_in_dim(halves, mine, 1, keepdims=False)
        send = lax.dynamic_index_in_dim(halves, 1 - mine, 1, keepdims=False)
        if bit == bits - 1:
            send = send.astype(jnp.bfloat16)
        flips = [(j, j ^ 1 << bit) for j in range(m)]
        partial = keep + lax.ppermute(send, "ch", flips).astype(jnp.float32)
    projected = partial.reshape(3, own, total).astype(jnp.bfloat16).astype(jnp.float32)

    taps = lax.dynamic_slice_in_dim(short_filter, place * own, own, 2)[:, :, :, None]
    padded = jnp.pad(projected, ((0, 0), (0, 0), (2, 0)))
    mixed = (
        taps[0] * projected + taps[1] * padded[:, :, 1 : total + 1] + taps[2] * padded[:, :, :total]
    )
    query = mixed[0]
    signal = (mixed[1] * mixed[2]).reshape(own, n, rows)

    response = lax.all_to_all(
        filter_spectrum.reshape(2, rows, n, own).transpose(2, 3, 0, 1),
        "ctx", split_axis=0, concat_axis=0, tiled=True,
    )
    grid = lax.broadcasted_iota(jnp.int32, (rows, rows), 0) * lax.broadcasted_iota(
        jnp.int32, (rows, rows), 1
    )
    local_cos, local_sin = phase_tables(grid % rows, rows)
    order = reverse_bits(lax.broadcasted_iota(jnp.int32, (n, 1), 0), sections)
    across = order * lax.broadcasted_iota(jnp.int32, (1, n), 1)
    across_cos, across_sin = phase_tables(across % n, n)
    turn = order * lax.broadcasted_iota(jnp.int32, (1, rows), 1)
    turn_cos, turn_sin = phase_tables(turn % total, total)
    turn_cos, turn_sin = turn_cos[:, None], turn_sin[:, None]
    real = product("rn,cnt->rct", across_cos, signal)
    imag = -product("rn,cnt->rct", across_sin, signal)
    real, imag = real * turn_cos + imag * turn_sin, imag * turn_cos - real * turn_sin
    spec_real = product("rct,tq->rcq", real, local_cos) + product("rct,tq->rcq", imag, local_sin)
    spec_imag = product("rct,tq->rcq", imag, local_cos) - product("rct,tq->rcq", real, local_sin)
    res_real, res_imag = response[:, :, 0], response[:, :, 1]
    prod_real = spec_real * res_real - spec_imag * res_imag
    prod_imag = spec_real * res_imag + spec_imag * res_real
    back_real = product("rcq,qt->rct", prod_real, local_cos) - product(
        "rcq,qt->rct", prod_imag, local_sin
    )
    back_imag = product("rcq,qt->rct", prod_imag, local_cos) + product(
        "rcq,qt->rct", prod_real, local_sin
    )
    back_real, back_imag = (
        back_real * turn_cos - back_imag * turn_sin,
        back_imag * turn_cos + back_real * turn_sin,
    )
    convolved = (
        product("rn,rct->cnt", across_cos, back_real)
        - product("rn,rct->cnt", across_sin, back_imag)
    ) / total
    gated = (query * convolved.reshape(own, total)).astype(jnp.bfloat16)

    out_rows = out_grad.shape[1] // n
    part = out_rows // m
    mine = lax.dynamic_index_in_dim(
        out_grad.reshape(rows, n, m, part), column, 2, keepdims=False
    )
    mine = lax.all_to_all(mine, "ctx", split_axis=1, concat_axis=0, tiled=True)
    grads = lax.all_gather(mine.reshape(total, part), "ch", axis=1, tiled=True)

    every = jnp.zeros((n // 2, 2, own, total), jnp.bfloat16)
    for index, low, high in gather_pairs(gated, n, place):
        every = lax.dynamic_update_slice(every, jnp.stack([low, high])[None], (index, 0, 0, 0))
    every = every.reshape(width, total)
    w_out_grad = lax.dot_general(
        grads, every, (((0,), (1,)), ((), ())), preferred_element_type=jnp.float32
    )
    out = lax.dynamic_slice_in_dim(every, place * rows, rows, 1).T
    return (out, w_out_grad)


def exact(left, right):
    return jnp.dot(left, right, precision=lax.Precision.HIGHEST, preferred_element_type=jnp.float32)

def tables(rows, lanes):
    grid = np.arange(rows)[:, None] * np.arange(rows)[None, :] % rows
    angle = 2.0 * math.pi / rows * grid
    table = np.zeros((rows, 2 * lanes), np.float32)
    table[:, :rows] = np.cos(angle)
    table[:, lanes : lanes + rows] = np.sin(angle)
    turn = 2.0 * math.pi / (8 * rows) * (np.arange(5)[:, None] * np.arange(rows)[None, :])
    return table, np.stack([np.cos(turn), np.sin(turn)]).astype(np.float32)

def convolve_kernel(odd_ref, mine_ref, other_ref, taps_ref, response_ref, table_ref, turn_ref, out_ref):
    own, total = out_ref.shape
    rows = total // 8
    lanes = table_ref.shape[1] // 2
    mine, other = mine_ref[...].astype(jnp.float32), other_ref[...].astype(jnp.float32)
    even, uneven = jnp.where(odd_ref[0] == 0, mine, other), jnp.where(odd_ref[0] == 0, other, mine)
    slabs = []
    for spot in range(4):
        slabs += [even[:, rows * spot : rows * (spot + 1)], uneven[:, rows * spot : rows * (spot + 1)]]
    projected = jnp.concatenate(slabs, axis=1)
    lane = lax.broadcasted_iota(jnp.int32, projected.shape, 1)
    mixed = taps_ref[0] * projected
    for back in (1, 2):
        moved = jnp.where(lane < back, 0.0, pltpu.roll(projected, back, 1))
        mixed += taps_ref[back] * moved
    query = mixed[:own]
    signal = mixed[own : 2 * own] * mixed[2 * own :]
    a = [signal[:, rows * i : rows * (i + 1)] for i in range(8)]
    half = math.sqrt(0.5)
    s04, d04, s26, d26 = a[0] + a[4], a[0] - a[4], a[2] + a[6], a[2] - a[6]
    s15, d15, s37, d37 = a[1] + a[5], a[1] - a[5], a[3] + a[7], a[3] - a[7]
    e, f = s04 + s26, s15 + s37
    g, h = half * (d15 - d37), half * (d15 + d37)
    real = [e + f, d04 + g, s04 - s26, d04 - g, e - f]
    imag = [None, -(d26 + h), s37 - s15, d26 - h, None]
    ins = [real[0]]
    for r in range(1, 5):
        cos, sin = turn_ref[0, r : r + 1], turn_ref[1, r : r + 1]
        if imag[r] is None:
            ins += [real[r] * cos, -real[r] * sin]
        else:
            ins += [real[r] * cos + imag[r] * sin, imag[r] * cos - real[r] * sin]
    spectrum = exact(jnp.concatenate(ins, axis=0), table_ref[...])
    response = [
        jnp.concatenate([response_ref[odd_ref[1 + r], i] for i in range(response_ref.shape[1])], axis=1)
        for r in range(8)
    ]
    response = [value.astype(jnp.float32) for value in response]
    outs = []
    for r in range(5):
        if r == 0:
            first = spectrum[:own]
            spec_real, spec_imag = first[:, :rows], -first[:, lanes : lanes + rows]
        else:
            first = spectrum[(2 * r - 1) * own : 2 * r * own]
            second = spectrum[2 * r * own : (2 * r + 1) * own]
            spec_real = first[:, :rows] + second[:, lanes : lanes + rows]
            spec_imag = second[:, :rows] - first[:, lanes : lanes + rows]
        own_class = response[r]
        res_real, res_imag = own_class[:, :rows], own_class[:, rows:]
        if r in (1, 2, 3):
            mirrored = response[8 - r]
            res_real = 0.5 * (res_real + mirrored[:, :rows])
            res_imag = 0.5 * (res_imag - mirrored[:, rows:])
        outs += [spec_real * res_real - spec_imag * res_imag, spec_real * res_imag + spec_imag * res_real]
    back = exact(jnp.concatenate(outs, axis=0), table_ref[...])
    u_real, u_imag = [], []
    for r in range(5):
        first = back[2 * r * own : (2 * r + 1) * own]
        second = back[(2 * r + 1) * own : (2 * r + 2) * own]
        v_real = first[:, :rows] - second[:, lanes : lanes + rows]
        if r == 0:
            u_real.append(v_real)
            u_imag.append(None)
            continue
        v_imag = second[:, :rows] + first[:, lanes : lanes + rows]
        cos, sin = turn_ref[0, r : r + 1], turn_ref[1, r : r + 1]
        u_real.append(v_real * cos - v_imag * sin)
        u_imag.append(None if r == 4 else v_imag * cos + v_real * sin)
    p, q = u_real[0] + u_real[4], u_real[0] - u_real[4]
    r13, i13 = u_real[1] + u_real[3], u_imag[1] - u_imag[3]
    dr, di = half * (u_real[1] - u_real[3]), half * (u_imag[1] + u_imag[3])
    two = 2.0
    r2, i2 = u_real[2], u_imag[2]
    y = [p + two * (r13 + r2), q + two * (dr - di - i2), p - two * (i13 + r2), q + two * (i2 - dr - di),
         p + two * (r2 - r13), q + two * (di - dr - i2), p + two * (i13 - r2), q + two * (dr + di + i2)]
    scale = 1.0 / total
    convolved = jnp.concatenate(y, axis=1) * scale
    out_ref[...] = (query * convolved).astype(jnp.bfloat16)

def convolve(odd, mine, other, taps, response):
    total = 2 * mine.shape[1]
    own = mine.shape[0] // 3
    rows = total // 8
    table, turn = tables(rows, -(-rows // 128) * 128)
    return pl.pallas_call(convolve_kernel, out_shape=jax.ShapeDtypeStruct((own, total), jnp.bfloat16),
        in_specs=[pl.BlockSpec(memory_space=pltpu.SMEM)] + [pl.BlockSpec(memory_space=pltpu.VMEM)] * 6,
        compiler_params=pltpu.CompilerParams(vmem_limit_bytes=48*2**20),
        cost_estimate=pl.CostEstimate(flops=10**9, bytes_accessed=4*10**6, transcendentals=0),
    )(odd, mine, other, taps, response, jnp.asarray(table), jnp.asarray(turn))


PARTS = 2


def pack_kernel(flag_ref, value_ref, grad_ref, out_ref):
    rows = value_ref.shape[1]
    n, _, count, lanes = out_ref.shape
    own = value_ref.shape[2] // n
    down = lax.broadcasted_iota(jnp.int32, (rows, rows), 0)
    along = lax.broadcasted_iota(jnp.int32, (rows, rows), 1)
    target = jnp.where(flag_ref[0] == 1, rows - 1 - down, down)
    swap = (along == target).astype(jnp.bfloat16)
    turned = [
        lax.dot_general(
            value_ref[part].astype(jnp.bfloat16),
            swap,
            (((0,), (0,)), ((), ())),
            preferred_element_type=jnp.float32,
        ).astype(jnp.bfloat16)
        for part in range(2)
    ]
    turned = jnp.concatenate(turned, axis=1)
    step = grad_ref.shape[1] // n
    for place in range(n):
        for chunk in range(count // own):
            out_ref[place, 0, own * chunk : own * (chunk + 1)] = turned[
                own * place : own * (place + 1), lanes * chunk : lanes * (chunk + 1)
            ]
        start = pl.multiple_of(place * step + flag_ref[1] * lanes, lanes)
        out_ref[place, 1] = grad_ref[:, pl.ds(start, lanes)]


def pack(flags, value, grad, n, m):
    rows = grad.shape[0]
    lanes = grad.shape[1] // (n * m)
    vmem = pl.BlockSpec(memory_space=pltpu.VMEM)
    return pl.pallas_call(
        pack_kernel,
        out_shape=jax.ShapeDtypeStruct((n, 2, rows, lanes), jnp.bfloat16),
        in_specs=[pl.BlockSpec(memory_space=pltpu.SMEM), vmem, vmem],
        out_specs=vmem,
        compiler_params=pltpu.CompilerParams(vmem_limit_bytes=32 * 2**20),
        cost_estimate=pl.CostEstimate(flops=10**8, bytes_accessed=4 * 2**20, transcendentals=0),
    )(flags, value, grad)


def cut_kernel(step, which_ref, value_ref, *outs):
    kinds, _, width = value_ref.shape
    size = width // len(outs)
    for index, out_ref in enumerate(outs):
        start = pl.multiple_of(which_ref[index] * size, size)
        for kind in range(kinds):
            piece = value_ref[kind, :, pl.ds(start, size)].T
            for group in range(size // step):
                place = group % PARTS * 2 + group // PARTS
                first = (place * kinds + kind) * step
                out_ref[first : first + step] = piece[group * step : (group + 1) * step]


def cut(step, which, value):
    kinds, deep, width = value.shape
    vmem = pl.BlockSpec(memory_space=pltpu.VMEM)
    count = which.shape[0]
    out = jax.ShapeDtypeStruct((kinds * width // count, deep), value.dtype)
    return pl.pallas_call(
        functools.partial(cut_kernel, step),
        out_shape=[out] * count,
        in_specs=[pl.BlockSpec(memory_space=pltpu.SMEM), vmem],
        out_specs=[vmem] * count,
        compiler_params=pltpu.CompilerParams(vmem_limit_bytes=32 * 2**20),
        cost_estimate=pl.CostEstimate(flops=0, bytes_accessed=3 * 2**20, transcendentals=0),
    )(which, value)


def fits(mesh):
    return mesh.shape["ctx"] == 8 and mesh.shape["ch"] == 4


def after(value, *others):
    return lax.optimization_barrier((value, *others))[0]


def special(features, w_in, short_filter, filter_spectrum, out_grad):
    n = lax.axis_size("ctx")
    m = lax.axis_size("ch")
    place = lax.axis_index("ctx")
    column = lax.axis_index("ch")
    rows, depth = features.shape
    total = rows * n
    share = n // m
    pairs = n // 2
    line = place // 2
    odd = place % 2
    block_depth = w_in.shape[0]
    width = w_in.shape[2]
    own = width // n
    sub = own // PARTS
    sections = n.bit_length() - 1
    flips = [(i, i ^ 1) for i in range(n)]
    shifts = [[(i, (i // 2 + s) % pairs * 2 + i % 2) for i in range(n)] for s in range(pairs)]
    up = [(i, i + 2) for i in range(n - 2)]
    down = [(i + 2, i) for i in range(n - 2)]

    def trade(value, bit):
        return lax.ppermute(value, "ch", [(j, j ^ 1 << bit) for j in range(m)])

    up1 = lax.ppermute(features, "ctx", up)
    down1 = lax.ppermute(features, "ctx", down)

    which = (column + jnp.arange(m, dtype=jnp.int32)) % m
    turned = cut(sub, which, w_in.transpose(1, 0, 2))
    pieces = []
    for step, piece in enumerate(turned):
        hops = []
        for i in range(n):
            for j in range(m):
                hops.append((i * m + j, ((j + step) % m * 2 + i % 2) * m + i // 2))
        if step == m - 1:
            piece = after(piece, up1, down1)
        pieces.append(lax.ppermute(piece, BOTH, hops))
    pieces += [lax.ppermute(piece, "ctx", flips) for piece in pieces]

    mirrored = (reverse_bits(place, sections) > n // 2).astype(jnp.int32)
    packed = pack(jnp.stack([mirrored, column]), filter_spectrum, out_grad, n, m)

    up2 = lax.ppermute(up1, "ctx", up)
    down2 = lax.ppermute(down1, "ctx", down)
    up3 = lax.ppermute(after(up2, packed), "ctx", up)
    down3 = lax.ppermute(after(down2, packed), "ctx", down)
    behind = [
        jnp.where(line >= 1, up1, down3),
        jnp.where(line >= 2, up2, down2),
        jnp.where(line >= 3, up3, down1),
    ]
    def along(value, *others):
        value = value.reshape(pairs, 2, *value.shape[1:])
        found = []
        for shift in range(pairs):
            piece = lax.dynamic_index_in_dim(value, (line - shift) % pairs, 0, keepdims=False)
            if shift:
                back = [(i, (i // 2 - shift) % pairs * 2 + i % 2) for i in range(n)]
                piece = lax.ppermute(after(piece, *others), "ctx", back)
            found.append(piece)
        return found


    whole = jnp.zeros((pairs, rows, depth), features.dtype)
    for shift, value in enumerate([features] + behind):
        value = jnp.where(
            odd == 0,
            value,
            jnp.concatenate([value[:, block_depth:], value[:, :block_depth]], axis=1),
        )
        whole = lax.dynamic_update_slice(whole, value[None], ((line - shift) % pairs, 0, 0))
    whole = whole.reshape(pairs * rows, depth)

    count = m // 2
    spot = 3 * 2 * sub
    weights = jnp.zeros((2, PARTS, count, spot, share * block_depth), w_in.dtype)
    for index, piece in enumerate(pieces):
        block, step = divmod(index, m)
        slot = (line - step) % m ^ column
        weights = lax.dynamic_update_slice(
            weights,
            piece.reshape(1, PARTS, 1, spot, block_depth),
            (slot % 2, 0, slot // 2, 0, block * block_depth),
        )

    def multiply(kind, part):
        left = weights[kind, part].reshape(count * spot, share * block_depth)
        result = lax.dot_general(
            left, whole, (((1,), (1,)), ((), ())), preferred_element_type=jnp.float32
        )
        return result.reshape(count, spot, -1)

    def beside(found, *others):
        found = jnp.stack([after(value, *others) for value in found])
        mine = lax.dynamic_index_in_dim(found, odd, 1, keepdims=False)
        give = lax.dynamic_index_in_dim(found, 1 - odd, 1, keepdims=False)
        return mine, lax.ppermute(give, "ctx", flips)

    order = jnp.asarray(ORDER, jnp.int32)
    places = (order % 2 ^ odd) * pairs + (order // 2 - line) % pairs
    places = jnp.concatenate([odd.reshape(1), places])

    taps = lax.dynamic_slice_in_dim(short_filter, place * own, own, 2)
    taps = taps.reshape(3, 3, PARTS, sub).transpose(2, 0, 1, 3).reshape(PARTS, 3, 3 * sub, 1)
    sends = [multiply(1, part) for part in range(PARTS)]
    keeps = [multiply(0, part) for part in range(PARTS)]
    gots = [trade(send, 0) for send in sends]
    onwards = [(keep[1] + got[1]).astype(jnp.bfloat16) for keep, got in zip(keeps, gots)]
    across = [trade(onward, 1) for onward in onwards]
    filters = along(packed[:, 0], *keeps)
    mine, other = beside(filters, onwards[0])
    response = jnp.concatenate([mine, other]).reshape(n, rows // own, own, -1)
    gated = []
    crossed = []
    gives = []
    for part in range(PARTS):
        projected = keeps[part][0] + gots[part][0] + after(across[part], *crossed).astype(jnp.float32)
        projected = projected.astype(jnp.bfloat16).reshape(2, 3 * sub, total // 2)
        mine = lax.dynamic_index_in_dim(projected, odd, 0, keepdims=False)
        give = lax.dynamic_index_in_dim(projected, 1 - odd, 0, keepdims=False)
        other = lax.ppermute(give, "ctx", flips)
        crossed.append(other)
        gives.append(give)
        gated.append(
            convolve(
                places, mine, other, taps[part],
                response[:, :, part * sub : (part + 1) * sub],
            )
        )

    mine, other = beside(along(packed[:, 1], *onwards), crossed[0], *gives)
    gates = [crossed, [other]]
    low, high = jnp.where(odd == 0, mine, other), jnp.where(odd == 0, other, mine)
    grads = jnp.stack([low, high], axis=1)
    grads = lax.dynamic_slice_in_dim(
        jnp.concatenate([grads, grads]), (pairs - line) % pairs, pairs, 0
    )
    grads = grads.reshape(total, grads.shape[3])
    for bit in (1, 0):
        other = trade(grads, bit)
        low = column >> bit & 1 == 0
        if bit == 1:
            grads = jnp.stack([jnp.where(low, grads, other), jnp.where(low, other, grads)])
        else:
            low, high = jnp.where(low, grads, other), jnp.where(low, other, grads)
            grads = jnp.concatenate([low[0], high[0], low[1], high[1]], axis=1)

    every = jnp.zeros((pairs, 2, PARTS, sub, total), jnp.bfloat16)
    for part in range(PARTS):
        near = [gated[part]]
        near += [lax.ppermute(gated[part], "ctx", shifts[s]) for s in range(1, pairs)]
        near = [after(value, *gates[part]) for value in near]
        near = jnp.stack(near)
        other = lax.ppermute(near, "ctx", flips)
        low = jnp.where(odd == 0, near, other)
        high = jnp.where(odd == 0, other, near)
        for shift in range(pairs):
            every = lax.dynamic_update_slice(
                every,
                jnp.stack([low[shift], high[shift]])[None, :, None],
                ((line - shift) % pairs, 0, part, 0, 0),
            )
    every = every.reshape(width, total)
    w_out_grad = lax.dot_general(
        grads, every, (((0,), (1,)), ((), ())), preferred_element_type=jnp.float32
    )
    out = lax.dynamic_slice_in_dim(every, place * rows, rows, 1).T
    return (out, w_out_grad)


def solution(mesh):
    in_specs = (
        P("ctx", "ch"),
        P("ctx", None, "ch"),
        P(None, None, "ch"),
        P(None, "ctx", "ch"),
        P("ctx", None),
    )
    out_specs = (P("ctx", "ch"), P("ctx", "ch"))
    on_device = special if fits(mesh) else general
    return jax.shard_map(
        on_device, mesh=mesh, in_specs=in_specs, out_specs=out_specs, check_vma=False
    )
```
